256 devices in a mesh: dp: 2 (over core), seq: 128 (over z, y, x).
Axes of the slice: x: 4, y: 4, z: 8, core: 2. Of those that a mesh axis runs over, the one named last changes fastest.
Arguments:
- query_tiles: bfloat16 [2, 128, 2, 64, 4096], P('dp', 'seq'), may hold values from -6 to 6
- key_tiles: bfloat16 [2, 128, 2, 64, 4096], P('dp', 'seq'), may hold values from -6 to 6
- value_tiles: bfloat16 [2, 128, 2, 64, 4096], P('dp', 'seq'), may hold values from -6 to 6
- cotangent: bfloat16 [2, 16384, 4096], P('dp', 'seq'), may hold values from -6 to 6
- filters: bfloat16 [128, 128], replicated, may hold values from -0.5 to 0.5
- doc_lengths: int32 [2, 8], replicated, may hold values from 1 to 8192, 16384 in all within a row
- arrival: int32 [2, 128, 2], P(None, 'seq'), may hold values from 0 to 1, as said below
Outputs:
- grad_query: bfloat16 [2, 128, 2, 64, 4096], P('dp', 'seq')
- grad_key: bfloat16 [2, 128, 2, 64, 4096], P('dp', 'seq')
- grad_value: bfloat16 [2, 128, 2, 64, 4096], P('dp', 'seq')
- grad_filters: float32 [128, 128], replicated
The draws below stay inside these ranges and needn't reach their ends.
Inputs may be any that keep to these rules, and one draw needn't show every extreme that they name: For every block s and sequence j, arrival[d, s, j] over all d is a permutation of 0 to 1.
All inputs are finite; a program needn't handle non-finite values.
Results may differ from the reference program's by a relative error of at most 0.005.
Values may be sent and summed in bfloat16 or wider, within the bound.
A program may use at most 192 MiB of HBM per device.

```python
import math
import jax
import jax.numpy as jnp
import numpy as np
from jax import lax

GROUPS = 128
GS = 32
KSIZE = 128
SLOT = 64
DOCS = 8
D = 4096
SEQLEN = 16384
N_DP = 2
N_SEQ = 128


def draw_arrival(key, part):
    key = jax.random.fold_in(key, 11)
    key_list = jax.random.split(key, N_SEQ * N_DP)
    orders = jax.vmap(lambda single: jax.random.permutation(single, N_DP))(key_list)
    return jnp.transpose(orders.reshape(N_SEQ, N_DP, N_DP), (2, 0, 1)).astype(jnp.int32)


def steps_of(rng, shape, cuts, smallest, top_value):
    def one(position, blocks):
        steps = jax.random.uniform(jax.random.fold_in(jax.random.fold_in(rng, 6), position), (blocks,), jnp.float32, smallest / len(cuts), top_value / len(cuts))
        return jnp.repeat(jnp.exp(steps), shape[position] // blocks).reshape((-1,) + (1,) * (len(shape) - position - 1))

    gain = one(*cuts[0])
    for cut in cuts[1:]:
        gain = gain * one(*cut)
    return gain


def profile(number_of, total, most, slope):
    weights = [(1 << 20) // math.isqrt(standing ** slope) + 1 for standing in range(2, number_of + 1)]
    spare, given = total - most - (number_of - 1), [1] * (number_of - 1)
    while spare > 0:
        candidates = [i for i in range(number_of - 1) if given[i] < most]
        pool, remaining = sum([weights[i] for i in candidates]), spare
        for i in candidates:
            extra = min(most - given[i], max(1, remaining * weights[i] // pool), spare)
            given[i] = given[i] + extra
            spare = spare - extra
    return np.array([most] + given)


def ragged(key, amount, total, reach, lean):
    if amount == 2:
        one = jax.random.randint(key, (), max(1, total - reach), min(reach, total - 1) + 1)
        return jnp.stack([one, total - one])
    lengths = jnp.asarray(profile(amount, total, reach, lean), jnp.int32)
    couples = (amount - 1) // 2
    giver, receiver = lengths[1:1 + 2 * couples:2], lengths[2:2 + 2 * couples:2]
    margin = jnp.minimum(giver - 1, reach - receiver)
    passed = jax.random.randint(jax.random.fold_in(key, 1), (couples,), 0, 1 << 20) % (margin + 1)
    lengths = lengths.at[1:1 + 2 * couples:2].set(giver - passed).at[2:2 + 2 * couples:2].set(receiver + passed)
    return lengths[jax.random.permutation(jax.random.fold_in(key, 2), amount)]


def normal_values(stream_key, dims, spread, limit, cuts=(), kind=jnp.bfloat16):
    gain = steps_of(stream_key, dims, cuts, -0.22, 0.18) if cuts else 1.0
    result = jax.random.normal(stream_key, dims, jnp.float32) * spread * gain
    return jnp.minimum(jnp.maximum(result, -limit), limit).astype(kind)


def setup_inputs(seed: int = 0) -> dict:
    splits = jax.random.split(jax.random.key(seed), 8)
    query_tiles = normal_values(splits[0], (N_DP, N_SEQ, N_DP, SLOT, D), 1.0, 6.0, ((0, 2), (1, 128)))
    key_tiles = normal_values(splits[1], (N_DP, N_SEQ, N_DP, SLOT, D), 1.0, 6.0, ((0, 2), (1, 128)))
    value_tiles = normal_values(splits[2], (N_DP, N_SEQ, N_DP, SLOT, D), 1.0, 6.0, ((0, 2), (1, 128)))
    cotangent = normal_values(splits[3], (N_DP, SEQLEN, D), 1.0, 6.0, ((0, 2), (1, 128)))
    filters = normal_values(splits[4], (GROUPS, KSIZE), KSIZE ** -0.5, 0.5)
    doc_lengths = jax.vmap(lambda own: ragged(own, DOCS, SEQLEN, SEQLEN // 2, 2))(jax.random.split(splits[5], N_DP)).reshape((N_DP, DOCS)).astype(jnp.int32)
    arrival = draw_arrival(jax.random.fold_in(splits[7], 71), 0)
    return {"query_tiles": query_tiles, "key_tiles": key_tiles, "value_tiles": value_tiles, "cotangent": cotangent, "filters": filters, "doc_lengths": doc_lengths, "arrival": arrival}


def doc_starts(positions, doc_lens):
    doc_ends = jnp.cumsum(doc_lens)
    return lax.optimization_barrier(jnp.sum(jnp.where(positions[:, None] >= doc_ends[None, :], doc_lens[None, :], 0), axis=1))

def reference(query_tiles, key_tiles, value_tiles, cotangent, filters, doc_lengths, arrival):
    onehot = (arrival[..., None] == jnp.arange(N_DP, dtype=jnp.int32)).astype(jnp.int32)
    inverse = lax.optimization_barrier(jnp.sum(jnp.arange(N_DP, dtype=jnp.int32)[:, None, None, None] * onehot, axis=0))
    seq_index = jnp.arange(N_SEQ, dtype=jnp.int32)[:, None, None]
    slot_index = jnp.arange(N_DP, dtype=jnp.int32)[None, :, None]

    def to_logical(stored):
        tiles = stored[inverse, seq_index, slot_index]
        return jnp.transpose(tiles, (1, 0, 2, 3, 4)).reshape(N_DP, SEQLEN, D)

    def to_stored(logical):
        tiles = logical.reshape(N_DP, N_SEQ, N_DP, SLOT, D)
        return tiles[jnp.arange(N_DP, dtype=jnp.int32)[None, None, :], jnp.arange(N_SEQ, dtype=jnp.int32)[None, :, None], arrival]
    queries = to_logical(query_tiles)
    keys_seq = to_logical(key_tiles)
    values_seq = to_logical(value_tiles)
    mixture = (keys_seq.astype(jnp.float32) * values_seq.astype(jnp.float32)).astype(jnp.bfloat16)
    gate_grad = (cotangent.astype(jnp.float32) * queries.astype(jnp.float32)).astype(jnp.bfloat16)
    block_rows = min(128, SEQLEN)
    span = block_rows + KSIZE
    block_count = SEQLEN // block_rows
    mix_pad = jnp.pad(mixture, ((0, 0), (KSIZE, KSIZE), (0, 0)))
    grad_pad = jnp.pad(gate_grad, ((0, 0), (KSIZE, KSIZE), (0, 0)))
    taps = filters.astype(jnp.float32)

    def block_terms(index):
        seq_id = index // block_count
        start_row = index % block_count * block_rows
        doc_lens = lax.dynamic_index_in_dim(doc_lengths, seq_id, 0, keepdims=False)
        mix_seq = lax.dynamic_index_in_dim(mix_pad, seq_id, 0, keepdims=False)
        grad_seq = lax.dynamic_index_in_dim(grad_pad, seq_id, 0, keepdims=False)
        window = lax.dynamic_slice_in_dim(mix_seq, start_row, span, 0).astype(jnp.float32).reshape(span, GROUPS, GS)
        grad_window = lax.dynamic_slice_in_dim(grad_seq, start_row + KSIZE, span, 0).astype(jnp.float32).reshape(span, GROUPS, GS)
        grad_rows = lax.dynamic_slice_in_dim(grad_seq, start_row + KSIZE, block_rows, 0).astype(jnp.float32).reshape(block_rows, GROUPS, GS)
        row_pos = start_row + jnp.arange(block_rows, dtype=jnp.int32)
        left_pos = start_row - KSIZE + jnp.arange(span, dtype=jnp.int32)
        right_pos = start_row + jnp.arange(span, dtype=jnp.int32)
        lag_fwd = row_pos[:, None] - left_pos[None, :]
        inside_fwd = (lag_fwd >= 0) & (lag_fwd < KSIZE) & (left_pos[None, :] >= doc_starts(row_pos, doc_lens)[:, None])
        weight_fwd = jnp.where(inside_fwd[None], taps[:, jnp.clip(lag_fwd, 0, KSIZE - 1)], 0.0)
        hidden = jnp.einsum('gte,egc->tgc', weight_fwd, window).reshape(block_rows, D)
        lag_back = right_pos[None, :] - row_pos[:, None]
        inside_back = (lag_back >= 0) & (lag_back < KSIZE) & (row_pos[:, None] >= doc_starts(right_pos, doc_lens)[None, :])
        weight_back = jnp.where(inside_back[None], taps[:, jnp.clip(lag_back, 0, KSIZE - 1)], 0.0)
        mix_grad = jnp.einsum('gpt,tgc->pgc', weight_back, grad_window).reshape(block_rows, D)
        correl = jnp.einsum('tgc,egc->gte', grad_rows, window) * inside_fwd.astype(jnp.float32)[None]
        skewed = jnp.pad(correl.reshape(GROUPS, block_rows * span), ((0, 0), (0, block_rows))).reshape(GROUPS, block_rows, span + 1)
        filter_terms = lax.optimization_barrier(jnp.sum(skewed[:, :, 1:KSIZE + 1], axis=1))[:, ::-1]
        flat_start = seq_id * SEQLEN + start_row
        cot_rows = lax.dynamic_slice_in_dim(cotangent.reshape(N_DP * SEQLEN, D), flat_start, block_rows, 0).astype(jnp.float32)
        key_rows = lax.dynamic_slice_in_dim(keys_seq.reshape(N_DP * SEQLEN, D), flat_start, block_rows, 0).astype(jnp.float32)
        value_rows = lax.dynamic_slice_in_dim(values_seq.reshape(N_DP * SEQLEN, D), flat_start, block_rows, 0).astype(jnp.float32)
        grad_q = (cot_rows * hidden).astype(jnp.bfloat16)
        grad_k = (mix_grad * value_rows).astype(jnp.bfloat16)
        grad_v = (mix_grad * key_rows).astype(jnp.bfloat16)
        return (grad_q, grad_k, grad_v, filter_terms)
    grad_q, grad_k, grad_v, filter_terms = lax.map(block_terms, jnp.arange(N_DP * block_count, dtype=jnp.int32))
    grad_query = to_stored(grad_q.reshape(N_DP, SEQLEN, D))
    grad_key = to_stored(grad_k.reshape(N_DP, SEQLEN, D))
    grad_value = to_stored(grad_v.reshape(N_DP, SEQLEN, D))
    grad_filters = lax.optimization_barrier(jnp.sum(filter_terms, axis=0)) * (1.0 / math.sqrt(N_DP * SEQLEN * GS))
    return (grad_query, grad_key, grad_value, grad_filters)
```

```python
import functools
import math

import jax
import jax.numpy as jnp
from jax import lax
from jax.experimental import pallas as pl
from jax.experimental.pallas import tpu as pltpu
from jax.sharding import PartitionSpec as P

MESH = pl.DeviceIdType.MESH
LANES = 128


def kernel_body(
    dims,
    chunks,
    inflight,
    scale,
    query_hbm,
    key_hbm,
    value_hbm,
    cot_hbm,
    filters_ref,
    doc_ref,
    arrival_ref,
    gq_hbm,
    gk_hbm,
    gv_hbm,
    gf_hbm,
    own,
    rcv,
    cot,
    mixx,
    ggx,
    taps_fwd,
    taps_back,
    rolled_fwd,
    rolled_back,
    masks_half,
    masks,
    diag,
    terms,
    stage_own,
    stage_oth,
    piece_one,
    piece_two,
    piece_three,
    own_sem,
    cot_sem,
    swap_send,
    swap_recv,
    mix_send,
    mix_recv,
    gg_send,
    gg_recv,
    out_sem,
    back_send,
    back_recv,
    one_send,
    one_recv,
    two_send,
    two_recv,
    three_send,
    three_recv,
    four_send,
    four_recv,
    final_sem,
):
    z_count, y_count, x_count = dims
    seq_count = z_count * y_count * x_count
    group_count, kernel = filters_ref.shape
    rows = kernel
    slot = own.shape[2]
    width = own.shape[3]
    tile_count = mixx.shape[0]
    per_chunk = tile_count // chunks
    per_tile = group_count // tile_count
    group_size = LANES // per_tile
    half_chunks = chunks // 2
    core = lax.axis_index("dp")
    other = 1 - core
    seq = lax.axis_index("seq")
    x = lax.rem(seq, x_count)
    y = lax.rem(lax.div(seq, x_count), y_count)
    z = lax.div(seq, x_count * y_count)
    sibling = (other, seq)
    following = (core, lax.rem(seq + 1, seq_count))
    previous = (core, lax.rem(seq + seq_count - 1, seq_count))
    team = 2 * x_count
    place = core * x_count + x

    def member(k):
        index = lax.rem(place + k, team)
        return index, (lax.div(index, x_count), seq - x + lax.rem(index, x_count))

    def along_y(k):
        index = lax.rem(y + k, y_count)
        return index, (core, seq + (index - y) * x_count)

    def along_z(k):
        index = lax.rem(z + k, z_count)
        return index, (core, seq + (index - z) * (x_count * y_count))

    def columns(c):
        return pl.ds(pl.multiple_of(c * width, width), width)

    sources = (key_hbm, value_hbm, query_hbm)

    def chunk_of(which, c):
        return chunks - 1 - c if which == 2 else c

    def own_copy(which, c):
        return pltpu.make_async_copy(
            sources[which].at[0, 0, core, :, columns(c)],
            own.at[which, c],
            own_sem.at[which, c],
        )

    def cot_copy(c):
        return pltpu.make_async_copy(cot_hbm.at[0, :, columns(c)], cot.at[c], cot_sem.at[c])

    def swap_copy(which, c):
        return pltpu.make_async_remote_copy(
            src_ref=sources[which].at[0, 0, other, :, columns(c)],
            dst_ref=rcv.at[which, c],
            send_sem=swap_send.at[which, c],
            recv_sem=swap_recv.at[which, c],
            device_id=sibling,
            device_id_type=MESH,
        )

    for c in range(chunks):
        for which in range(3):
            own_copy(which, chunk_of(which, c)).start()
        cot_copy(chunks - 1 - c).start()

    barrier = pltpu.get_barrier_semaphore()
    partners = [sibling, following, previous]
    partners += [member(k)[1] for k in range(1, team)]
    partners += [along_y(k)[1] for k in range(1, y_count)]
    partners += [along_z(k)[1] for k in range(1, z_count)]
    for partner in partners:
        pl.semaphore_signal(barrier, inc=1, device_id=partner, device_id_type=MESH)

    square = (rows, rows)
    row = lax.broadcasted_iota(jnp.int32, square, 0)
    col = lax.broadcasted_iota(jnp.int32, square, 1)
    first = seq * rows

    def doc_start(position):
        end = jnp.int32(0)
        result = jnp.zeros(square, jnp.int32)
        for i in range(doc_ref.shape[1]):
            length = doc_ref[core, i]
            end = end + length
            result = result + jnp.where(position >= end, length, 0)
        return result

    def as_mask(condition):
        return jnp.where(condition, 1.0, 0.0).astype(jnp.float32)

    start_row = doc_start(first + row)
    start_col = doc_start(first + col)
    start_far = doc_start(first + rows + col)
    built = (
        as_mask((col > row) & (first - rows + col >= start_row)),
        as_mask((col <= row) & (first + col >= start_row)),
        as_mask((col >= row) & (first + row >= start_col)),
        as_mask((col < row) & (first + row >= start_far)),
    )
    for i, mask in enumerate(built):
        masks[i] = mask
        masks_half[i] = mask.astype(jnp.bfloat16)

    flip = as_mask(lax.rem(row + col, kernel) == 0)

    pl.semaphore_wait(barrier, len(partners))
    for c in range(chunks):
        for which in range(3):
            swap_copy(which, chunk_of(which, c)).start()

    straight = filters_ref[...].astype(jnp.float32)
    turned = jnp.dot(
        filters_ref[...], flip.astype(jnp.bfloat16), preferred_element_type=jnp.float32
    )
    for s in range(8):
        rolled_fwd[pl.ds(s, group_count, stride=8), :] = pltpu.roll(turned, s, 1)
        rolled_back[pl.ds(s, group_count, stride=8), :] = pltpu.roll(straight, s, 1)

    held = arrival_ref[core, 0, core]
    own_first = jnp.full((slot, LANES), held, jnp.int32) == 0

    def in_order(mine, received):
        return jnp.concatenate(
            [jnp.where(own_first, mine, received), jnp.where(own_first, received, mine)], axis=0
        )

    def halo_mix(c):
        tiles = pl.ds(c * per_chunk, per_chunk)
        return pltpu.make_async_remote_copy(
            src_ref=mixx.at[tiles, pl.ds(rows, rows), :],
            dst_ref=mixx.at[tiles, pl.ds(0, rows), :],
            send_sem=mix_send.at[c],
            recv_sem=mix_recv.at[c],
            device_id=following,
            device_id_type=MESH,
        )

    def halo_gg(c):
        tiles = pl.ds(c * per_chunk, per_chunk)
        return pltpu.make_async_remote_copy(
            src_ref=ggx.at[tiles, pl.ds(0, rows), :],
            dst_ref=ggx.at[tiles, pl.ds(rows, rows), :],
            send_sem=gg_send.at[c],
            recv_sem=gg_recv.at[c],
            device_id=previous,
            device_id_type=MESH,
        )

    def assemble(c, carry):
        back = chunks - 1 - c
        for which in range(2):
            own_copy(which, c).wait()
            swap_copy(which, c).wait_recv()
        for q in range(per_chunk):
            lanes = slice(q * LANES, (q + 1) * LANES)
            mine = own[0, c, :, lanes].astype(jnp.float32) * own[1, c, :, lanes].astype(jnp.float32)
            received = rcv[0, c, :, lanes].astype(jnp.float32) * rcv[1, c, :, lanes].astype(
                jnp.float32
            )
            mixx[c * per_chunk + q, rows:, :] = in_order(mine, received).astype(jnp.bfloat16)

        @pl.when(c < inflight)
        def _():
            halo_mix(c).start()

        own_copy(2, back).wait()
        swap_copy(2, back).wait_recv()
        cot_copy(back).wait()
        for q in range(per_chunk):
            lanes = slice(q * LANES, (q + 1) * LANES)
            gate = in_order(
                own[2, back, :, lanes].astype(jnp.float32),
                rcv[2, back, :, lanes].astype(jnp.float32),
            )
            ggx[back * per_chunk + q, :rows, :] = (
                gate * cot[back, :, lanes].astype(jnp.float32)
            ).astype(jnp.bfloat16)

        @pl.when(c < inflight)
        def _():
            halo_gg(back).start()

        return carry

    lax.fori_loop(0, chunks, assemble, 0)

    def band(g, carry):
        base = pl.multiple_of(g * rows, rows)
        eight = pl.ds(pl.multiple_of(g * 8, 8), 8)
        for rolled, out, near, far in (
            (rolled_fwd, taps_fwd, 0, 1),
            (rolled_back, taps_back, 2, 3),
        ):
            start = rolled[eight, :]
            whole = jnp.concatenate(
                [start if k == 0 else pltpu.roll(start, 8 * k, 1) for k in range(rows // 8)],
                axis=0,
            ).astype(jnp.bfloat16)
            out[pl.ds(base, rows), :rows] = whole * masks_half[near]
            out[pl.ds(base, rows), rows:] = whole * masks_half[far]
        return carry

    lax.fori_loop(0, group_count, band, 0, unroll=2)

    lane_group = lax.div(lax.broadcasted_iota(jnp.int32, square, 1), group_size)

    def pick(parts):
        result = parts[:rows]
        for j in range(1, per_tile):
            result = jnp.where(lane_group == j, parts[j * rows : (j + 1) * rows], result)
        return result

    def spread(block):
        return jnp.concatenate(
            [
                block * jnp.where(lane_group == j, 1.0, 0.0).astype(jnp.bfloat16)
                for j in range(per_tile)
            ],
            axis=0,
        )

    def split(result):
        top, bottom = result[:slot], result[slot:]
        return jnp.where(own_first, top, bottom), jnp.where(own_first, bottom, top)

    def correlate(tile, left, right, near, far):
        product = lax.dot_general(
            spread(left), right, (((1,), (1,)), ((), ())), preferred_element_type=jnp.float32
        )
        for j in range(per_tile):
            total = None
            for k in range(rows // 8):
                here = slice(j * rows + 8 * k, j * rows + 8 * k + 8)
                mask_rows = slice(8 * k, 8 * k + 8)
                part = (
                    product[here, :rows] * masks[near, mask_rows]
                    + product[here, rows:] * masks[far, mask_rows]
                )
                if k:
                    part = pltpu.roll(part, rows - 8 * k, 1)
                total = part if total is None else total + part
            diag[pl.ds(pl.multiple_of((tile * per_tile + j) * 8, 8), 8), :] = total

    def forward(c, q, with_terms):
        tile = c * per_chunk + q
        lanes = pl.ds(pl.multiple_of(q * LANES, LANES), LANES)
        window = mixx[tile]
        lhs = taps_fwd[pl.ds(pl.multiple_of(tile * per_tile * rows, rows), per_tile * rows), :]
        hidden = pick(jnp.dot(lhs, window, preferred_element_type=jnp.float32))
        mine, theirs = split(cot[c, :, lanes].astype(jnp.float32) * hidden)
        stage_own[2, c, :, lanes] = mine.astype(jnp.bfloat16)
        stage_oth[2, c, :, lanes] = theirs.astype(jnp.bfloat16)
        if with_terms:
            correlate(tile, ggx[tile, :rows, :], window, 0, 1)

    def backward(c, q, with_terms):
        tile = c * per_chunk + q
        lanes = pl.ds(pl.multiple_of(q * LANES, LANES), LANES)
        window = ggx[tile]
        lhs = taps_back[pl.ds(pl.multiple_of(tile * per_tile * rows, rows), per_tile * rows), :]
        grad = pick(jnp.dot(lhs, window, preferred_element_type=jnp.float32))
        mine, theirs = split(grad)
        for which in range(2):
            factor = 1 - which
            stage_own[which, c, :, lanes] = (
                mine * own[factor, c, :, lanes].astype(jnp.float32)
            ).astype(jnp.bfloat16)
            stage_oth[which, c, :, lanes] = (
                theirs * rcv[factor, c, :, lanes].astype(jnp.float32)
            ).astype(jnp.bfloat16)
        if with_terms:
            correlate(tile, mixx[tile, rows:, :], window, 2, 3)

    results = (gk_hbm, gv_hbm, gq_hbm)

    def out_copy(which, c):
        return pltpu.make_async_copy(
            stage_own.at[which, c],
            results[which].at[0, 0, core, :, columns(c)],
            out_sem.at[which, c],
        )

    def back_copy(which, c):
        return pltpu.make_async_remote_copy(
            src_ref=stage_oth.at[which, c],
            dst_ref=results[which].at[0, 0, core, :, columns(c)],
            send_sem=back_send.at[which, c],
            recv_sem=back_recv.at[which, c],
            device_id=sibling,
            device_id_type=MESH,
        )

    def step(c, with_terms):
        back = chunks - 1 - c
        halo_mix(c).wait_recv()
        halo_gg(back).wait_recv()

        @pl.when(c + inflight < chunks)
        def _():
            halo_mix(c + inflight).start()
            halo_gg(back - inflight).start()

        def inner(q, carry):
            forward(c, q, with_terms)
            backward(back, q, with_terms)
            return carry

        lax.fori_loop(0, per_chunk, inner, 0)
        for which, chunk in ((2, c), (0, back), (1, back)):
            out_copy(which, chunk).start()
            back_copy(which, chunk).start()

    def step_with_terms(c, carry):
        step(c, True)
        return carry

    lax.fori_loop(0, half_chunks, step_with_terms, 0)

    reversed_half = group_count // 2
    sums = None
    for s in range(8):
        part = diag[pl.ds(s, group_count, stride=8), :]
        if s:
            part = pltpu.roll(part, rows - s, 1)
        sums = part if sums is None else sums + part
    terms[:reversed_half, :] = jnp.dot(
        sums[:reversed_half],
        flip,
        precision=lax.Precision.HIGHEST,
        preferred_element_type=jnp.float32,
    )
    terms[reversed_half:, :] = sums[reversed_half:]
    piece = group_count // team

    def piece_rows(index):
        return pl.ds(pl.multiple_of(index * piece, piece), piece)

    def remote(src, dst, send, recv, device):
        return pltpu.make_async_remote_copy(
            src_ref=src,
            dst_ref=dst,
            send_sem=send,
            recv_sem=recv,
            device_id=device,
            device_id_type=MESH,
        )

    def exchange(ring, count, here, buffer, source, send, recv):
        copies = []
        for k in range(1, count):
            index, device = ring(k)
            copy = remote(
                source(index), buffer.at[here], send.at[k - 1], recv.at[k - 1], device
            )
            copy.start()
            copies.append(copy)
        return copies

    def arrive(ring, count, buffer, send, recv):
        for k in range(1, count):
            index, device = ring(count - k)
            remote(
                buffer.at[index], buffer.at[index], send.at[k - 1], recv.at[k - 1], device
            ).wait_recv()

    def total_of(buffer, count):
        total = buffer[0]
        for k in range(1, count):
            total = total + buffer[k]
        return total

    sent = []
    piece_one[place] = terms[piece_rows(place), :]
    sent += exchange(
        member, team, place, piece_one, lambda i: terms.at[piece_rows(i)], one_send, one_recv
    )

    stages = [0, 1, 2, 3]

    def advance(stage):
        if stage == 0:
            arrive(member, team, piece_one, one_send, one_recv)
            piece_two[y] = total_of(piece_one, team)
            return exchange(
                along_y, y_count, y, piece_two, lambda i: piece_two.at[y], two_send, two_recv
            )
        if stage == 1:
            arrive(along_y, y_count, piece_two, two_send, two_recv)
            piece_three[z] = total_of(piece_two, y_count)
            return exchange(
                along_z, z_count, z, piece_three, lambda i: piece_three.at[z], three_send, three_recv
            )
        if stage == 2:
            arrive(along_z, z_count, piece_three, three_send, three_recv)
            diag[piece_rows(place), :] = total_of(piece_three, z_count) * scale
            copies = []
            for k in range(1, team):
                index, device = member(k)
                copy = remote(
                    diag.at[piece_rows(place)],
                    diag.at[piece_rows(place)],
                    four_send.at[k - 1],
                    four_recv.at[k - 1],
                    device,
                )
                copy.start()
                copies.append(copy)
            return copies
        for k in range(1, team):
            index, device = member(team - k)
            remote(
                diag.at[piece_rows(index)],
                diag.at[piece_rows(index)],
                four_send.at[k - 1],
                four_recv.at[k - 1],
                device,
            ).wait_recv()
        return []

    for c in range(half_chunks, chunks):
        step(c, False)
        if stages:
            sent += advance(stages.pop(0))
    while stages:
        sent += advance(stages.pop(0))
    final = pltpu.make_async_copy(diag.at[pl.ds(0, group_count)], gf_hbm, final_sem)
    final.start()

    for copy in sent:
        copy.wait_send()

    def finish(c, carry):
        halo_mix(c).wait_send()
        halo_gg(c).wait_send()
        for which in range(3):
            swap_copy(which, c).wait_send()
            out_copy(which, c).wait()
            back_copy(which, c).wait()
        return carry

    lax.fori_loop(0, chunks, finish, 0)
    final.wait()


def body(dims, chunks, inflight, *operands):
    query_tiles, cotangent, filters = operands[0], operands[3], operands[4]
    slot, features = query_tiles.shape[3:]
    rows = cotangent.shape[1]
    groups = filters.shape[0]
    z_count, y_count, x_count = dims
    team = 2 * x_count
    piece = groups // team
    width = features // chunks
    tiles = features // LANES
    half, single = jnp.bfloat16, jnp.float32
    total = 2 * rows * z_count * y_count * x_count * (features // groups)
    anywhere = pl.BlockSpec(memory_space=pl.ANY)
    dma = pltpu.SemaphoreType.DMA
    return pl.pallas_call(
        functools.partial(kernel_body, dims, chunks, inflight, 1.0 / math.sqrt(total)),
        out_shape=(
            jax.ShapeDtypeStruct(query_tiles.shape, half),
            jax.ShapeDtypeStruct(query_tiles.shape, half),
            jax.ShapeDtypeStruct(query_tiles.shape, half),
            jax.ShapeDtypeStruct(filters.shape, single),
        ),
        in_specs=[anywhere] * 4
        + [
            pl.BlockSpec(memory_space=pltpu.VMEM),
            pl.BlockSpec(memory_space=pltpu.SMEM),
            pl.BlockSpec(memory_space=pltpu.SMEM),
        ],
        out_specs=[anywhere] * 4,
        scratch_shapes=[
            pltpu.VMEM((3, chunks, slot, width), half),
            pltpu.VMEM((3, chunks, slot, width), half),
            pltpu.VMEM((chunks, rows, width), half),
            pltpu.VMEM((tiles, 2 * rows, LANES), half),
            pltpu.VMEM((tiles, 2 * rows, LANES), half),
            pltpu.VMEM((groups * rows, 2 * rows), half),
            pltpu.VMEM((groups * rows, 2 * rows), half),
            pltpu.VMEM((groups * 8, rows), single),
            pltpu.VMEM((groups * 8, rows), single),
            pltpu.VMEM((4, rows, rows), half),
            pltpu.VMEM((4, rows, rows), single),
            pltpu.VMEM((groups * 8, rows), single),
            pltpu.VMEM((groups, rows), single),
            pltpu.VMEM((3, chunks, slot, width), half),
            pltpu.VMEM((3, chunks, slot, width), half),
            pltpu.VMEM((team, piece, rows), single),
            pltpu.VMEM((y_count, piece, rows), single),
            pltpu.VMEM((z_count, piece, rows), single),
            dma((3, chunks)),
            dma((chunks,)),
            dma((3, chunks)),
            dma((3, chunks)),
            dma((chunks,)),
            dma((chunks,)),
            dma((chunks,)),
            dma((chunks,)),
            dma((3, chunks)),
            dma((3, chunks)),
            dma((3, chunks)),
            dma((team - 1,)),
            dma((team - 1,)),
            dma((y_count - 1,)),
            dma((y_count - 1,)),
            dma((z_count - 1,)),
            dma((z_count - 1,)),
            dma((team - 1,)),
            dma((team - 1,)),
            dma,
        ],
        compiler_params=pltpu.CompilerParams(
            collective_id=0, has_side_effects=True, vmem_limit_bytes=48 * 1024 * 1024
        ),
        cost_estimate=pl.CostEstimate(
            flops=12 * rows * rows * features, bytes_accessed=14 * rows * features, transcendentals=0
        ),
    )(*operands)


def build(mesh, dims, chunks, inflight):
    placed = (
        P("dp", "seq", None, None, None),
        P("dp", "seq", None, None, None),
        P("dp", "seq", None, None, None),
        P("dp", "seq", None),
        P(),
        P(),
        P(None, "seq", None),
    )
    return jax.shard_map(
        functools.partial(body, dims, chunks, inflight),
        mesh=mesh,
        in_specs=placed,
        out_specs=(
            P("dp", "seq", None, None, None),
            P("dp", "seq", None, None, None),
            P("dp", "seq", None, None, None),
            P(),
        ),
        check_vma=False,
    )


def solution(mesh):
    return build(mesh, (8, 4, 4), 8, 8)
```

```python
import functools
import math

import jax
import jax.numpy as jnp
from jax import lax
from jax.experimental import pallas as pl
from jax.experimental.pallas import tpu as pltpu
from jax.sharding import PartitionSpec as P

MESH = pl.DeviceIdType.MESH
LANES = 128
VMEM_BYTES = 60 * 1024 * 1024


def kernel_body(
    dims,
    chunks,
    scale,
    query_hbm,
    key_hbm,
    value_hbm,
    cot_hbm,
    filters_hbm,
    doc_hbm,
    arrival_hbm,
    gq_hbm,
    gk_hbm,
    gv_hbm,
    gf_hbm,
    filters_ref,
    doc_ref,
    arrival_ref,
    own,
    rcv,
    cot,
    mixx,
    ggx,
    taps_fwd,
    taps_back,
    rolled_fwd,
    rolled_back,
    masks_half,
    masks,
    diag,
    terms,
    stage_own,
    stage_oth,
    piece_one,
    piece_two,
    piece_three,
    small_sem,
    own_sem,
    swap_send,
    swap_recv,
    mix_send,
    mix_recv,
    gg_send,
    gg_recv,
    out_sem,
    back_send,
    back_recv,
    one_send,
    one_recv,
    two_send,
    two_recv,
    three_send,
    three_recv,
    four_send,
    four_recv,
    final_sem,
):
    z_count, y_count, x_count = dims
    seq_count = z_count * y_count * x_count
    group_count, kernel = filters_ref.shape
    rows = kernel
    slot = rcv.shape[2]
    width = rcv.shape[3]
    tile_count = mixx.shape[0]
    per_chunk = tile_count // chunks
    per_tile = group_count // tile_count
    group_size = LANES // per_tile
    half_chunks = chunks // 2
    core = lax.axis_index("dp")
    other = 1 - core
    seq = lax.axis_index("seq")
    x = lax.rem(seq, x_count)
    y = lax.rem(lax.div(seq, x_count), y_count)
    z = lax.div(seq, x_count * y_count)
    sibling = (other, seq)
    following = (core, lax.rem(seq + 1, seq_count))
    previous = (core, lax.rem(seq + seq_count - 1, seq_count))
    team = 2 * x_count
    place = core * x_count + x

    def member(k):
        index = lax.rem(place + k, team)
        return index, (lax.div(index, x_count), seq - x + lax.rem(index, x_count))

    def along_y(k):
        index = lax.rem(y + k, y_count)
        return index, (core, seq + (index - y) * x_count)

    def along_z(k):
        index = lax.rem(z + k, z_count)
        return index, (core, seq + (index - z) * (x_count * y_count))

    def columns(c):
        return pl.ds(pl.multiple_of(c * width, width), width)

    barrier = pltpu.get_barrier_semaphore()
    partners = [sibling, following, previous]
    partners += [member(k)[1] for k in range(1, team)]
    partners += [along_y(k)[1] for k in range(1, y_count)]
    partners += [along_z(k)[1] for k in range(1, z_count)]
    for partner in partners:
        pl.semaphore_signal(barrier, inc=1, device_id=partner, device_id_type=MESH)

    small = [
        pltpu.make_async_copy(doc_hbm, doc_ref, small_sem.at[0]),
        pltpu.make_async_copy(filters_hbm, filters_ref, small_sem.at[1]),
        pltpu.make_async_copy(arrival_hbm, arrival_ref, small_sem.at[2]),
    ]
    for copy in small:
        copy.start()

    sources = (key_hbm, value_hbm, query_hbm)

    def chunk_of(which, c):
        return chunks - 1 - c if which == 2 else c

    own_copies = [
        pltpu.make_async_copy(sources[which].at[0, 0, core], own.at[which], own_sem.at[which])
        for which in range(3)
    ]
    own_copies.append(pltpu.make_async_copy(cot_hbm.at[0], cot, own_sem.at[3]))
    for copy in own_copies:
        copy.start()

    def swap_copy(which, c):
        return pltpu.make_async_remote_copy(
            src_ref=sources[which].at[0, 0, other, :, columns(c)],
            dst_ref=rcv.at[which, c],
            send_sem=swap_send.at[which, c],
            recv_sem=swap_recv.at[which, c],
            device_id=sibling,
            device_id_type=MESH,
        )

    pl.semaphore_wait(barrier, len(partners))

    def swap(c):
        for which in range(3):
            swap_copy(which, chunk_of(which, c)).start()

    ahead = 2
    for c in range(ahead):
        swap(c)
    for copy in small:
        copy.wait()

    square = (rows, rows)
    row = lax.broadcasted_iota(jnp.int32, square, 0)
    col = lax.broadcasted_iota(jnp.int32, square, 1)
    first = seq * rows

    def doc_start(position):
        end = jnp.int32(0)
        result = jnp.zeros(square, jnp.int32)
        for i in range(doc_ref.shape[1]):
            length = doc_ref[core, i]
            end = end + length
            result = result + jnp.where(position >= end, length, 0)
        return result

    def as_mask(condition):
        return jnp.where(condition, 1.0, 0.0).astype(jnp.float32)

    start_row = doc_start(first + row)
    start_col = doc_start(first + col)
    start_far = doc_start(first + rows + col)
    built = (
        as_mask((col > row) & (first - rows + col >= start_row)),
        as_mask((col <= row) & (first + col >= start_row)),
        as_mask((col >= row) & (first + row >= start_col)),
        as_mask((col < row) & (first + row >= start_far)),
    )
    for i, mask in enumerate(built):
        masks[i] = mask
        masks_half[i] = mask.astype(jnp.bfloat16)

    flip = as_mask(lax.rem(row + col, kernel) == 0)

    straight = filters_ref[...].astype(jnp.float32)
    turned = jnp.dot(
        filters_ref[...], flip.astype(jnp.bfloat16), preferred_element_type=jnp.float32
    )
    for s in range(8):
        rolled_fwd[pl.ds(s, group_count, stride=8), :] = pltpu.roll(turned, s, 1)
        rolled_back[pl.ds(s, group_count, stride=8), :] = pltpu.roll(straight, s, 1)

    for copy in own_copies:
        copy.wait()

    held = arrival_ref[core, 0, core]
    own_first = jnp.full((slot, LANES), held, jnp.int32) == 0

    def in_order(mine, received):
        return jnp.concatenate(
            [jnp.where(own_first, mine, received), jnp.where(own_first, received, mine)], axis=0
        )

    def halo_mix(c):
        tiles = pl.ds(c * per_chunk, per_chunk)
        return pltpu.make_async_remote_copy(
            src_ref=mixx.at[tiles, pl.ds(rows, rows), :],
            dst_ref=mixx.at[tiles, pl.ds(0, rows), :],
            send_sem=mix_send.at[c],
            recv_sem=mix_recv.at[c],
            device_id=following,
            device_id_type=MESH,
        )

    def halo_gg(c):
        tiles = pl.ds(c * per_chunk, per_chunk)
        return pltpu.make_async_remote_copy(
            src_ref=ggx.at[tiles, pl.ds(0, rows), :],
            dst_ref=ggx.at[tiles, pl.ds(rows, rows), :],
            send_sem=gg_send.at[c],
            recv_sem=gg_recv.at[c],
            device_id=previous,
            device_id_type=MESH,
        )

    def halos(c):
        halo_mix(c).start()
        halo_gg(chunks - 1 - c).start()

    def lanes_of(c, q):
        return pl.ds(pl.multiple_of(c * width + q * LANES, LANES), LANES)

    early = 3 * chunks // 4

    def assemble(c, carry):
        back = chunks - 1 - c

        @pl.when(c + ahead < chunks)
        def _():
            swap(c + ahead)

        for which in range(2):
            swap_copy(which, c).wait_recv()
        for q in range(per_chunk):
            lanes = slice(q * LANES, (q + 1) * LANES)
            here = lanes_of(c, q)
            mine = own[0, :, here].astype(jnp.float32) * own[1, :, here].astype(jnp.float32)
            received = rcv[0, c, :, lanes].astype(jnp.float32) * rcv[1, c, :, lanes].astype(
                jnp.float32
            )
            mixx[c * per_chunk + q, rows:, :] = in_order(mine, received).astype(jnp.bfloat16)

        @pl.when(c < early)
        def _():
            halo_mix(c).start()

        swap_copy(2, back).wait_recv()
        for q in range(per_chunk):
            lanes = slice(q * LANES, (q + 1) * LANES)
            here = lanes_of(back, q)
            gate = in_order(
                own[2, :, here].astype(jnp.float32), rcv[2, back, :, lanes].astype(jnp.float32)
            )
            ggx[back * per_chunk + q, :rows, :] = (
                gate * cot[:, here].astype(jnp.float32)
            ).astype(jnp.bfloat16)

        @pl.when(c < early)
        def _():
            halo_gg(back).start()

        return carry

    lax.fori_loop(0, chunks, assemble, 0)

    def band(g, carry):
        base = pl.multiple_of(g * rows, rows)
        eight = pl.ds(pl.multiple_of(g * 8, 8), 8)
        for rolled, out, near, far in (
            (rolled_fwd, taps_fwd, 0, 1),
            (rolled_back, taps_back, 2, 3),
        ):
            start = rolled[eight, :]
            whole = jnp.concatenate(
                [start if k == 0 else pltpu.roll(start, 8 * k, 1) for k in range(rows // 8)],
                axis=0,
            ).astype(jnp.bfloat16)
            out[pl.ds(base, rows), :rows] = whole * masks_half[near]
            out[pl.ds(base, rows), rows:] = whole * masks_half[far]
        return carry

    lax.fori_loop(0, group_count, band, 0, unroll=8)

    lane_group = lax.div(lax.broadcasted_iota(jnp.int32, square, 1), group_size)

    def pick(parts):
        result = parts[:rows]
        for j in range(1, per_tile):
            result = jnp.where(lane_group == j, parts[j * rows : (j + 1) * rows], result)
        return result

    def spread(block):
        return jnp.concatenate(
            [
                block * jnp.where(lane_group == j, 1.0, 0.0).astype(jnp.bfloat16)
                for j in range(per_tile)
            ],
            axis=0,
        )

    def split(result):
        top, bottom = result[:slot], result[slot:]
        return jnp.where(own_first, top, bottom), jnp.where(own_first, bottom, top)

    def correlate(tile, left, right, near, far):
        product = lax.dot_general(
            spread(left), right, (((1,), (1,)), ((), ())), preferred_element_type=jnp.float32
        )
        for j in range(per_tile):
            total = None
            for k in range(rows // 8):
                here = slice(j * rows + 8 * k, j * rows + 8 * k + 8)
                mask_rows = slice(8 * k, 8 * k + 8)
                part = (
                    product[here, :rows] * masks[near, mask_rows]
                    + product[here, rows:] * masks[far, mask_rows]
                )
                if k:
                    part = pltpu.roll(part, rows - 8 * k, 1)
                total = part if total is None else total + part
            diag[pl.ds(pl.multiple_of((tile * per_tile + j) * 8, 8), 8), :] = total

    def forward(c, q):
        tile = c * per_chunk + q
        lanes = pl.ds(pl.multiple_of(q * LANES, LANES), LANES)
        lhs = taps_fwd[pl.ds(pl.multiple_of(tile * per_tile * rows, rows), per_tile * rows), :]
        hidden = pick(jnp.dot(lhs, mixx[tile], preferred_element_type=jnp.float32))
        mine, theirs = split(cot[:, lanes_of(c, q)].astype(jnp.float32) * hidden)
        stage_own[2, c, :, lanes] = mine.astype(jnp.bfloat16)
        stage_oth[2, c, :, lanes] = theirs.astype(jnp.bfloat16)

    def backward(c, q):
        tile = c * per_chunk + q
        lanes = pl.ds(pl.multiple_of(q * LANES, LANES), LANES)
        lhs = taps_back[pl.ds(pl.multiple_of(tile * per_tile * rows, rows), per_tile * rows), :]
        grad = pick(jnp.dot(lhs, ggx[tile], preferred_element_type=jnp.float32))
        mine, theirs = split(grad)
        for which in range(2):
            factor = 1 - which
            stage_own[which, c, :, lanes] = (
                mine * own[factor, :, lanes_of(c, q)].astype(jnp.float32)
            ).astype(jnp.bfloat16)
            stage_oth[which, c, :, lanes] = (
                theirs * rcv[factor, c, :, lanes].astype(jnp.float32)
            ).astype(jnp.bfloat16)

    results = (gk_hbm, gv_hbm, gq_hbm)

    def out_copy(which, c):
        return pltpu.make_async_copy(
            stage_own.at[which, c],
            results[which].at[0, 0, core, :, columns(c)],
            out_sem.at[which, c],
        )

    def back_copy(which, c):
        return pltpu.make_async_remote_copy(
            src_ref=stage_oth.at[which, c],
            dst_ref=results[which].at[0, 0, core, :, columns(c)],
            send_sem=back_send.at[which, c],
            recv_sem=back_recv.at[which, c],
            device_id=sibling,
            device_id_type=MESH,
        )

    def arrived(c):
        halo_mix(c).wait_recv()
        halo_gg(chunks - 1 - c).wait_recv()

    def terms_step(c, carry):
        back = chunks - 1 - c
        arrived(c)

        def inner(q, inner_carry):
            tile = c * per_chunk + q
            correlate(tile, ggx[tile, :rows, :], mixx[tile], 0, 1)
            tile = back * per_chunk + q
            correlate(tile, mixx[tile, rows:, :], ggx[tile], 2, 3)
            return inner_carry

        lax.fori_loop(0, per_chunk, inner, 0, unroll=True)
        return carry

    def step(c, carry):
        back = chunks - 1 - c

        @pl.when(c >= half_chunks)
        def _():
            arrived(c)

        def inner(q, inner_carry):
            forward(c, q)
            backward(back, q)
            return inner_carry

        lax.fori_loop(0, per_chunk, inner, 0, unroll=True)
        for which, chunk in ((2, c), (0, back), (1, back)):
            out_copy(which, chunk).start()
            back_copy(which, chunk).start()
        return carry

    before = chunks // 4
    lax.fori_loop(0, half_chunks - 1, terms_step, 0)
    lax.fori_loop(0, before, step, 0)
    terms_step(half_chunks - 1, 0)

    reversed_half = group_count // 2
    sums = None
    for s in range(8):
        part = diag[pl.ds(s, group_count, stride=8), :]
        if s:
            part = pltpu.roll(part, rows - s, 1)
        sums = part if sums is None else sums + part
    terms[:reversed_half, :] = jnp.dot(
        sums[:reversed_half],
        flip,
        precision=lax.Precision.HIGHEST,
        preferred_element_type=jnp.float32,
    )
    terms[reversed_half:, :] = sums[reversed_half:]
    piece = group_count // team

    def piece_rows(index):
        return pl.ds(pl.multiple_of(index * piece, piece), piece)

    def remote(src, dst, send, recv, device):
        return pltpu.make_async_remote_copy(
            src_ref=src,
            dst_ref=dst,
            send_sem=send,
            recv_sem=recv,
            device_id=device,
            device_id_type=MESH,
        )

    def exchange(ring, count, here, buffer, source, send, recv):
        copies = []
        for k in range(1, count):
            index, device = ring(k)
            copy = remote(
                source(index), buffer.at[here], send.at[k - 1], recv.at[k - 1], device
            )
            copy.start()
            copies.append(copy)
        return copies

    def arrive(ring, count, buffer, send, recv):
        for k in range(1, count):
            index, device = ring(count - k)
            remote(
                buffer.at[index], buffer.at[index], send.at[k - 1], recv.at[k - 1], device
            ).wait_recv()

    def total_of(buffer, count):
        total = buffer[0]
        for k in range(1, count):
            total = total + buffer[k]
        return total

    own_piece = pltpu.make_async_copy(
        diag.at[piece_rows(place)], gf_hbm.at[piece_rows(place)], final_sem
    )
    sent = []
    piece_one[place] = terms[piece_rows(place), :]
    sent += exchange(
        member, team, place, piece_one, lambda i: terms.at[piece_rows(i)], one_send, one_recv
    )

    middle = (
        (along_z, z_count, z, piece_three, three_send, three_recv),
        (along_y, y_count, y, piece_two, two_send, two_recv),
    )

    def advance(stage):
        if stage == 0:
            arrive(member, team, piece_one, one_send, one_recv)
            ring, count, here, buffer, send, recv = middle[0]
            buffer[here] = total_of(piece_one, team)
            return exchange(ring, count, here, buffer, lambda i: buffer.at[here], send, recv)
        if stage == 1:
            ring, count, here, buffer, send, recv = middle[0]
            arrive(ring, count, buffer, send, recv)
            total = total_of(buffer, count)
            ring, count, here, buffer, send, recv = middle[1]
            buffer[here] = total
            return exchange(ring, count, here, buffer, lambda i: buffer.at[here], send, recv)
        if stage == 2:
            ring, count, here, buffer, send, recv = middle[1]
            arrive(ring, count, buffer, send, recv)
            diag[piece_rows(place), :] = total_of(buffer, count) * scale
            own_piece.start()
            copies = []
            for k in range(1, team):
                index, device = member(k)
                copy = remote(
                    diag.at[piece_rows(place)],
                    gf_hbm.at[piece_rows(place)],
                    four_send.at[k - 1],
                    four_recv.at[k - 1],
                    device,
                )
                copy.start()
                copies.append(copy)
            return copies
        for k in range(1, team):
            index, device = member(team - k)
            remote(
                gf_hbm.at[piece_rows(index)],
                gf_hbm.at[piece_rows(index)],
                four_send.at[k - 1],
                four_recv.at[k - 1],
                device,
            ).wait_recv()
        return []

    middle_chunk = (early + chunks) // 2
    late = [early, middle_chunk, middle_chunk, chunks]
    ends = [before, chunks // 2, 5 * chunks // 8, 7 * chunks // 8, chunks]
    for stage in range(4):
        if stage < 3:
            for c in range(late[stage], late[stage + 1]):
                halos(c)
        lax.fori_loop(ends[stage], ends[stage + 1], step, 0)
        sent += advance(stage)

    for copy in sent:
        copy.wait_send()

    def finish(c, carry):
        halo_mix(c).wait_send()
        halo_gg(c).wait_send()
        for which in range(3):
            swap_copy(which, c).wait_send()
            out_copy(which, c).wait()
            back_copy(which, c).wait()
        return carry

    lax.fori_loop(0, chunks, finish, 0)
    own_piece.wait()


def hand_over(count, *refs):
    copies = []
    for i in range(count):
        source, target, sems = refs[i], refs[count + i], refs[-1]
        if len(source.shape) == 2:
            copies.append(pltpu.make_async_copy(source, target, sems.at[2 * i]))
            continue
        for j in range(2):
            copies.append(
                pltpu.make_async_copy(
                    source.at[0, 0, j], target.at[0, 0, j], sems.at[2 * i + j]
                )
            )
    for copy in copies:
        copy.start()
    for copy in copies:
        copy.wait()


def body(dims, chunks, *operands):
    query_tiles, cotangent, filters = operands[0], operands[3], operands[4]
    slot, features = query_tiles.shape[3:]
    rows = cotangent.shape[1]
    groups = filters.shape[0]
    z_count, y_count, x_count = dims
    team = 2 * x_count
    piece = groups // team
    width = features // chunks
    tiles = features // LANES
    half, single = jnp.bfloat16, jnp.float32
    total = 2 * rows * z_count * y_count * x_count * (features // groups)
    anywhere = pl.BlockSpec(memory_space=pl.ANY)
    dma = pltpu.SemaphoreType.DMA
    results = pl.pallas_call(
        functools.partial(kernel_body, dims, chunks, 1.0 / math.sqrt(total)),
        out_shape=(
            pltpu.VMEM(query_tiles.shape, half),
            pltpu.VMEM(query_tiles.shape, half),
            pltpu.VMEM(query_tiles.shape, half),
            pltpu.VMEM(filters.shape, single),
        ),
        in_specs=[anywhere] * 7,
        out_specs=[anywhere] * 4,
        scratch_shapes=[
            pltpu.VMEM(filters.shape, half),
            pltpu.SMEM(operands[5].shape, jnp.int32),
            pltpu.SMEM(operands[6].shape, jnp.int32),
            pltpu.VMEM((3, slot, features), half),
            pltpu.VMEM((3, chunks, slot, width), half),
            pltpu.VMEM((rows, features), half),
            pltpu.VMEM((tiles, 2 * rows, LANES), half),
            pltpu.VMEM((tiles, 2 * rows, LANES), half),
            pltpu.VMEM((groups * rows, 2 * rows), half),
            pltpu.VMEM((groups * rows, 2 * rows), half),
            pltpu.VMEM((groups * 8, rows), single),
            pltpu.VMEM((groups * 8, rows), single),
            pltpu.VMEM((4, rows, rows), half),
            pltpu.VMEM((4, rows, rows), single),
            pltpu.VMEM((groups * 8, rows), single),
            pltpu.VMEM((groups, rows), single),
            pltpu.VMEM((3, chunks, slot, width), half),
            pltpu.VMEM((3, chunks, slot, width), half),
            pltpu.VMEM((team, piece, rows), single),
            pltpu.VMEM((y_count, piece, rows), single),
            pltpu.VMEM((z_count, piece, rows), single),
            dma((3,)),
            dma((4,)),
            dma((3, chunks)),
            dma((3, chunks)),
            dma((chunks,)),
            dma((chunks,)),
            dma((chunks,)),
            dma((chunks,)),
            dma((3, chunks)),
            dma((3, chunks)),
            dma((3, chunks)),
            dma((team - 1,)),
            dma((team - 1,)),
            dma((y_count - 1,)),
            dma((y_count - 1,)),
            dma((z_count - 1,)),
            dma((z_count - 1,)),
            dma((team - 1,)),
            dma((team - 1,)),
            dma,
        ],
        compiler_params=pltpu.CompilerParams(
            collective_id=0, has_side_effects=True, vmem_limit_bytes=VMEM_BYTES
        ),
        cost_estimate=pl.CostEstimate(
            flops=12 * rows * rows * features, bytes_accessed=14 * rows * features, transcendentals=0
        ),
    )(*operands)
    count = len(results)
    return pl.pallas_call(
        functools.partial(hand_over, count),
        out_shape=tuple(jax.ShapeDtypeStruct(r.shape, r.dtype) for r in results),
        in_specs=[anywhere] * count,
        out_specs=[anywhere] * count,
        scratch_shapes=[dma((2 * count,))],
        compiler_params=pltpu.CompilerParams(vmem_limit_bytes=2 * 1024 * 1024),
    )(*results)


def build(mesh, dims, chunks):
    placed = (
        P("dp", "seq", None, None, None),
        P("dp", "seq", None, None, None),
        P("dp", "seq", None, None, None),
        P("dp", "seq", None),
        P(),
        P(),
        P(None, "seq", None),
    )
    return jax.shard_map(
        functools.partial(body, dims, chunks),
        mesh=mesh,
        in_specs=placed,
        out_specs=(
            P("dp", "seq", None, None, None),
            P("dp", "seq", None, None, None),
            P("dp", "seq", None, None, None),
            P(),
        ),
        check_vma=False,
    )


def solution(mesh):
    return build(mesh, (8, 4, 4), 8)
```

```python
import functools
import math

import jax
import jax.numpy as jnp
from jax import lax
from jax.experimental import pallas as pl
from jax.experimental.pallas import tpu as pltpu
from jax.sharding import PartitionSpec as P

MESH = pl.DeviceIdType.MESH
LANES = 128
VMEM_BYTES = 60 * 1024 * 1024


def kernel_body(
    dims,
    chunks,
    scale,
    query_hbm,
    key_hbm,
    value_hbm,
    cot_hbm,
    filters_hbm,
    doc_hbm,
    arrival_hbm,
    gq_hbm,
    gk_hbm,
    gv_hbm,
    gf_hbm,
    filters_ref,
    doc_ref,
    arrival_ref,
    own,
    rcv,
    cot,
    mixx,
    ggx,
    taps_fwd,
    taps_back,
    rolled_fwd,
    rolled_back,
    masks_half,
    masks,
    diag,
    terms,
    stage_own,
    stage_oth,
    piece_one,
    piece_two,
    piece_three,
    small_sem,
    own_sem,
    swap_send,
    swap_recv,
    mix_send,
    mix_recv,
    gg_send,
    gg_recv,
    out_sem,
    back_send,
    back_recv,
    one_send,
    one_recv,
    two_send,
    two_recv,
    three_send,
    three_recv,
    four_send,
    four_recv,
    final_sem,
):
    z_count, y_count, x_count = dims
    seq_count = z_count * y_count * x_count
    group_count, kernel = filters_ref.shape
    rows = kernel
    slot = rcv.shape[2]
    width = rcv.shape[3]
    tile_count = mixx.shape[0]
    per_chunk = tile_count // chunks
    per_tile = group_count // tile_count
    group_size = LANES // per_tile
    half_chunks = chunks // 2
    core = lax.axis_index("dp")
    other = 1 - core
    seq = lax.axis_index("seq")
    x = lax.rem(seq, x_count)
    y = lax.rem(lax.div(seq, x_count), y_count)
    z = lax.div(seq, x_count * y_count)
    sibling = (other, seq)
    following = (core, lax.rem(seq + 1, seq_count))
    previous = (core, lax.rem(seq + seq_count - 1, seq_count))
    team = 2 * x_count
    place = core * x_count + x

    def member(k, back=False):
        steps = k % x_count
        here_x = lax.rem(x + (x_count - steps if back else steps), x_count)
        here_core = core if k < x_count else other
        return here_core * x_count + here_x, (here_core, seq - x + here_x)

    def along_y(k, back=False):
        index = lax.rem(y + (y_count - k if back else k), y_count)
        return index, (core, seq + (index - y) * x_count)

    def along_z(k, back=False):
        index = lax.rem(z + (z_count - k if back else k), z_count)
        return index, (core, seq + (index - z) * (x_count * y_count))

    def order(ring, count):
        around = x_count if ring is member else count
        return sorted(range(1, count), key=lambda k: -min(k % around, -k % around))

    def columns(c):
        return pl.ds(pl.multiple_of(c * width, width), width)

    barrier = pltpu.get_barrier_semaphore()
    partners = [along_z(k)[1] for k in order(along_z, z_count)]
    partners += [following, previous]
    partners += [along_y(k)[1] for k in order(along_y, y_count)]
    partners += [member(k)[1] for k in order(member, team)]
    partners += [sibling]
    for partner in partners:
        pl.semaphore_signal(barrier, inc=1, device_id=partner, device_id_type=MESH)

    small = [
        pltpu.make_async_copy(doc_hbm, doc_ref, small_sem.at[0]),
        pltpu.make_async_copy(filters_hbm, filters_ref, small_sem.at[1]),
        pltpu.make_async_copy(arrival_hbm, arrival_ref, small_sem.at[2]),
    ]
    for copy in small:
        copy.start()

    sources = (key_hbm, value_hbm, query_hbm)

    def chunk_of(which, c):
        return chunks - 1 - c if which == 2 else c

    own_copies = [
        pltpu.make_async_copy(sources[which].at[0, 0, core], own.at[which], own_sem.at[which])
        for which in range(3)
    ]
    own_copies.append(pltpu.make_async_copy(cot_hbm.at[0], cot, own_sem.at[3]))
    for copy in own_copies:
        copy.start()

    def swap_copy(which, c):
        return pltpu.make_async_remote_copy(
            src_ref=sources[which].at[0, 0, other, :, columns(c)],
            dst_ref=rcv.at[which, c],
            send_sem=swap_send.at[which, c],
            recv_sem=swap_recv.at[which, c],
            device_id=sibling,
            device_id_type=MESH,
        )

    pl.semaphore_wait(barrier, len(partners))

    def swap(c):
        for which in range(3):
            swap_copy(which, chunk_of(which, c)).start()

    ahead = 2
    for c in range(ahead):
        swap(c)
    for copy in small:
        copy.wait()

    square = (rows, rows)
    row = lax.broadcasted_iota(jnp.int32, square, 0)
    col = lax.broadcasted_iota(jnp.int32, square, 1)
    first = seq * rows

    def doc_start(position):
        end = jnp.int32(0)
        result = jnp.zeros(square, jnp.int32)
        for i in range(doc_ref.shape[1]):
            length = doc_ref[core, i]
            end = end + length
            result = result + jnp.where(position >= end, length, 0)
        return result

    def as_mask(condition):
        return jnp.where(condition, 1.0, 0.0).astype(jnp.float32)

    start_row = doc_start(first + row)
    start_col = doc_start(first + col)
    start_far = doc_start(first + rows + col)
    built = (
        as_mask((col > row) & (first - rows + col >= start_row)),
        as_mask((col <= row) & (first + col >= start_row)),
        as_mask((col >= row) & (first + row >= start_col)),
        as_mask((col < row) & (first + row >= start_far)),
    )
    for i, mask in enumerate(built):
        masks[i] = mask
        masks_half[i] = mask.astype(jnp.bfloat16)

    flip = as_mask(lax.rem(row + col, kernel) == 0)

    straight = filters_ref[...].astype(jnp.float32)
    turned = jnp.dot(
        filters_ref[...], flip.astype(jnp.bfloat16), preferred_element_type=jnp.float32
    )
    for s in range(8):
        rolled_fwd[pl.ds(s, group_count, stride=8), :] = pltpu.roll(turned, s, 1)
        rolled_back[pl.ds(s, group_count, stride=8), :] = pltpu.roll(straight, s, 1)

    for copy in own_copies:
        copy.wait()

    held = arrival_ref[core, 0, core]
    own_first = jnp.full((slot, LANES), held, jnp.int32) == 0

    def in_order(mine, received):
        return jnp.concatenate(
            [jnp.where(own_first, mine, received), jnp.where(own_first, received, mine)], axis=0
        )

    def halo_mix(c):
        tiles = pl.ds(c * per_chunk, per_chunk)
        return pltpu.make_async_remote_copy(
            src_ref=mixx.at[tiles, pl.ds(rows, rows), :],
            dst_ref=mixx.at[tiles, pl.ds(0, rows), :],
            send_sem=mix_send.at[c],
            recv_sem=mix_recv.at[c],
            device_id=following,
            device_id_type=MESH,
        )

    def halo_gg(c):
        tiles = pl.ds(c * per_chunk, per_chunk)
        return pltpu.make_async_remote_copy(
            src_ref=ggx.at[tiles, pl.ds(0, rows), :],
            dst_ref=ggx.at[tiles, pl.ds(rows, rows), :],
            send_sem=gg_send.at[c],
            recv_sem=gg_recv.at[c],
            device_id=previous,
            device_id_type=MESH,
        )

    mix_turns = (x == x_count - 1) & (y == y_count - 1)
    gg_turns = (x == 0) & (y == 0)

    def halos(first, last, turning):
        @pl.when(mix_turns == turning)
        def _():
            for c in range(first, last):
                halo_mix(c).start()

        @pl.when(gg_turns == turning)
        def _():
            for c in range(first, last):
                halo_gg(chunks - 1 - c).start()

    def lanes_of(c, q):
        return pl.ds(pl.multiple_of(c * width + q * LANES, LANES), LANES)

    plain = (3 * chunks // 4, 7 * chunks // 8, chunks, chunks)
    turned = (3 * chunks // 4, 7 * chunks // 8, 7 * chunks // 8, chunks)

    def assemble(c, carry):
        back = chunks - 1 - c

        @pl.when(c + ahead < chunks)
        def _():
            swap(c + ahead)

        for which in range(2):
            swap_copy(which, c).wait_recv()
        for q in range(per_chunk):
            lanes = slice(q * LANES, (q + 1) * LANES)
            here = lanes_of(c, q)
            mine = own[0, :, here].astype(jnp.float32) * own[1, :, here].astype(jnp.float32)
            received = rcv[0, c, :, lanes].astype(jnp.float32) * rcv[1, c, :, lanes].astype(
                jnp.float32
            )
            mixx[c * per_chunk + q, rows:, :] = in_order(mine, received).astype(jnp.bfloat16)

        @pl.when(c < jnp.where(mix_turns, turned[0], plain[0]))
        def _():
            halo_mix(c).start()

        swap_copy(2, back).wait_recv()
        for q in range(per_chunk):
            lanes = slice(q * LANES, (q + 1) * LANES)
            here = lanes_of(back, q)
            gate = in_order(
                own[2, :, here].astype(jnp.float32), rcv[2, back, :, lanes].astype(jnp.float32)
            )
            ggx[back * per_chunk + q, :rows, :] = (
                gate * cot[:, here].astype(jnp.float32)
            ).astype(jnp.bfloat16)

        @pl.when(c < jnp.where(gg_turns, turned[0], plain[0]))
        def _():
            halo_gg(back).start()

        return carry

    lax.fori_loop(0, chunks, assemble, 0)

    def band(g, carry):
        base = pl.multiple_of(g * rows, rows)
        eight = pl.ds(pl.multiple_of(g * 8, 8), 8)
        for rolled, out, near, far in (
            (rolled_fwd, taps_fwd, 0, 1),
            (rolled_back, taps_back, 2, 3),
        ):
            start = rolled[eight, :]
            whole = jnp.concatenate(
                [start if k == 0 else pltpu.roll(start, 8 * k, 1) for k in range(rows // 8)],
                axis=0,
            ).astype(jnp.bfloat16)
            out[pl.ds(base, rows), :rows] = whole * masks_half[near]
            out[pl.ds(base, rows), rows:] = whole * masks_half[far]
        return carry

    lax.fori_loop(0, group_count, band, 0, unroll=8)

    lane_group = lax.div(lax.broadcasted_iota(jnp.int32, square, 1), group_size)

    def pick(parts):
        result = parts[:rows]
        for j in range(1, per_tile):
            result = jnp.where(lane_group == j, parts[j * rows : (j + 1) * rows], result)
        return result

    def spread(block):
        return jnp.concatenate(
            [
                block * jnp.where(lane_group == j, 1.0, 0.0).astype(jnp.bfloat16)
                for j in range(per_tile)
            ],
            axis=0,
        )

    def split(result):
        top, bottom = result[:slot], result[slot:]
        return jnp.where(own_first, top, bottom), jnp.where(own_first, bottom, top)

    def correlate(tile, left, right, near, far):
        product = lax.dot_general(
            spread(left), right, (((1,), (1,)), ((), ())), preferred_element_type=jnp.float32
        )
        for j in range(per_tile):
            total = None
            for k in range(rows // 8):
                here = slice(j * rows + 8 * k, j * rows + 8 * k + 8)
                mask_rows = slice(8 * k, 8 * k + 8)
                part = (
                    product[here, :rows] * masks[near, mask_rows]
                    + product[here, rows:] * masks[far, mask_rows]
                )
                if k:
                    part = pltpu.roll(part, rows - 8 * k, 1)
                total = part if total is None else total + part
            diag[pl.ds(pl.multiple_of((tile * per_tile + j) * 8, 8), 8), :] = total

    def forward(c, q):
        tile = c * per_chunk + q
        lanes = pl.ds(pl.multiple_of(q * LANES, LANES), LANES)
        lhs = taps_fwd[pl.ds(pl.multiple_of(tile * per_tile * rows, rows), per_tile * rows), :]
        hidden = pick(jnp.dot(lhs, mixx[tile], preferred_element_type=jnp.float32))
        mine, theirs = split(cot[:, lanes_of(c, q)].astype(jnp.float32) * hidden)
        stage_own[2, c, :, lanes] = mine.astype(jnp.bfloat16)
        stage_oth[2, c, :, lanes] = theirs.astype(jnp.bfloat16)

    def backward(c, q):
        tile = c * per_chunk + q
        lanes = pl.ds(pl.multiple_of(q * LANES, LANES), LANES)
        lhs = taps_back[pl.ds(pl.multiple_of(tile * per_tile * rows, rows), per_tile * rows), :]
        grad = pick(jnp.dot(lhs, ggx[tile], preferred_element_type=jnp.float32))
        mine, theirs = split(grad)
        for which in range(2):
            factor = 1 - which
            stage_own[which, c, :, lanes] = (
                mine * own[factor, :, lanes_of(c, q)].astype(jnp.float32)
            ).astype(jnp.bfloat16)
            stage_oth[which, c, :, lanes] = (
                theirs * rcv[factor, c, :, lanes].astype(jnp.float32)
            ).astype(jnp.bfloat16)

    results = (gk_hbm, gv_hbm, gq_hbm)

    def out_copy(which, c):
        return pltpu.make_async_copy(
            stage_own.at[which, c],
            results[which].at[0, 0, core, :, columns(c)],
            out_sem.at[which, c],
        )

    def back_copy(which, c):
        return pltpu.make_async_remote_copy(
            src_ref=stage_oth.at[which, c],
            dst_ref=results[which].at[0, 0, core, :, columns(c)],
            send_sem=back_send.at[which, c],
            recv_sem=back_recv.at[which, c],
            device_id=sibling,
            device_id_type=MESH,
        )

    def arrived(c):
        halo_mix(c).wait_recv()
        halo_gg(chunks - 1 - c).wait_recv()

    def terms_step(c, carry):
        back = chunks - 1 - c
        arrived(c)

        def inner(q, inner_carry):
            tile = c * per_chunk + q
            correlate(tile, ggx[tile, :rows, :], mixx[tile], 0, 1)
            tile = back * per_chunk + q
            correlate(tile, mixx[tile, rows:, :], ggx[tile], 2, 3)
            return inner_carry

        lax.fori_loop(0, per_chunk, inner, 0, unroll=True)
        return carry

    def step(c, carry):
        back = chunks - 1 - c

        @pl.when(c >= half_chunks)
        def _():
            arrived(c)

        def inner(q, inner_carry):
            forward(c, q)
            backward(back, q)
            return inner_carry

        lax.fori_loop(0, per_chunk, inner, 0, unroll=True)
        for which, chunk in ((2, c), (0, back), (1, back)):
            out_copy(which, chunk).start()
            back_copy(which, chunk).start()
        return carry

    before = chunks // 4
    lax.fori_loop(0, half_chunks - 1, terms_step, 0)
    lax.fori_loop(0, before, step, 0)
    terms_step(half_chunks - 1, 0)

    reversed_half = group_count // 2
    sums = None
    for s in range(8):
        part = diag[pl.ds(s, group_count, stride=8), :]
        if s:
            part = pltpu.roll(part, rows - s, 1)
        sums = part if sums is None else sums + part
    terms[:reversed_half, :] = jnp.dot(
        sums[:reversed_half],
        flip,
        precision=lax.Precision.HIGHEST,
        preferred_element_type=jnp.float32,
    )
    terms[reversed_half:, :] = sums[reversed_half:]
    piece = group_count // team

    def piece_rows(index):
        return pl.ds(pl.multiple_of(index * piece, piece), piece)

    def remote(src, dst, send, recv, device):
        return pltpu.make_async_remote_copy(
            src_ref=src,
            dst_ref=dst,
            send_sem=send,
            recv_sem=recv,
            device_id=device,
            device_id_type=MESH,
        )

    def exchange(ring, count, here, buffer, source, send, recv):
        copies = []
        for k in order(ring, count):
            index, device = ring(k)
            copy = remote(
                source(index), buffer.at[here], send.at[k - 1], recv.at[k - 1], device
            )
            copy.start()
            copies.append(copy)
        return copies

    def arrive(ring, count, buffer, send, recv):
        for k in range(1, count):
            index, device = ring(k, back=True)
            remote(
                buffer.at[index], buffer.at[index], send.at[k - 1], recv.at[k - 1], device
            ).wait_recv()

    def total_of(buffer, count):
        total = buffer[0]
        for k in range(1, count):
            total = total + buffer[k]
        return total

    own_piece = pltpu.make_async_copy(
        diag.at[piece_rows(place)], gf_hbm.at[piece_rows(place)], final_sem
    )
    sent = []
    piece_one[place] = terms[piece_rows(place), :]
    sent += exchange(
        member, team, place, piece_one, lambda i: terms.at[piece_rows(i)], one_send, one_recv
    )

    middle = (
        (along_z, z_count, z, piece_three, three_send, three_recv),
        (along_y, y_count, y, piece_two, two_send, two_recv),
    )

    def advance(stage):
        if stage == 0:
            arrive(member, team, piece_one, one_send, one_recv)
            ring, count, here, buffer, send, recv = middle[0]
            buffer[here] = total_of(piece_one, team)
            return exchange(ring, count, here, buffer, lambda i: buffer.at[here], send, recv)
        if stage == 1:
            ring, count, here, buffer, send, recv = middle[0]
            arrive(ring, count, buffer, send, recv)
            total = total_of(buffer, count)
            ring, count, here, buffer, send, recv = middle[1]
            buffer[here] = total
            return exchange(ring, count, here, buffer, lambda i: buffer.at[here], send, recv)
        if stage == 2:
            ring, count, here, buffer, send, recv = middle[1]
            arrive(ring, count, buffer, send, recv)
            diag[piece_rows(place), :] = total_of(buffer, count) * scale
            own_piece.start()
            copies = []
            for k in order(member, team):
                index, device = member(k)
                copy = remote(
                    diag.at[piece_rows(place)],
                    gf_hbm.at[piece_rows(place)],
                    four_send.at[k - 1],
                    four_recv.at[k - 1],
                    device,
                )
                copy.start()
                copies.append(copy)
            return copies
        for k in range(1, team):
            index, device = member(k, back=True)
            remote(
                gf_hbm.at[piece_rows(index)],
                gf_hbm.at[piece_rows(index)],
                four_send.at[k - 1],
                four_recv.at[k - 1],
                device,
            ).wait_recv()
        return []


    def finish(c, carry):
        halo_mix(c).wait_send()
        halo_gg(c).wait_send()
        for which in range(3):
            swap_copy(which, c).wait_send()
            out_copy(which, c).wait()
            back_copy(which, c).wait()
        return carry

    ends = (before, chunks // 2, 5 * chunks // 8, 7 * chunks // 8, chunks)
    for stage in range(4):
        if stage < 3:
            halos(plain[stage], plain[stage + 1], False)
            halos(turned[stage], turned[stage + 1], True)
        lax.fori_loop(ends[stage], ends[stage + 1], step, 0)
        if stage == 3:
            for copy in sent[: -(team - 1)]:
                copy.wait_send()
            lax.fori_loop(0, chunks, finish, 0)
        sent += advance(stage)
    for copy in sent[-(team - 1) :]:
        copy.wait_send()
    own_piece.wait()


def hand_over(count, *refs):
    copies = []
    for i in range(count):
        source, target, sems = refs[i], refs[count + i], refs[-1]
        if len(source.shape) == 2:
            copies.append(pltpu.make_async_copy(source, target, sems.at[2 * i]))
            continue
        for j in range(2):
            copies.append(
                pltpu.make_async_copy(
                    source.at[0, 0, j], target.at[0, 0, j], sems.at[2 * i + j]
                )
            )
    for copy in copies:
        copy.start()
    for copy in copies:
        copy.wait()


def body(dims, chunks, *operands):
    query_tiles, cotangent, filters = operands[0], operands[3], operands[4]
    slot, features = query_tiles.shape[3:]
    rows = cotangent.shape[1]
    groups = filters.shape[0]
    z_count, y_count, x_count = dims
    team = 2 * x_count
    piece = groups // team
    width = features // chunks
    tiles = features // LANES
    half, single = jnp.bfloat16, jnp.float32
    total = 2 * rows * z_count * y_count * x_count * (features // groups)
    anywhere = pl.BlockSpec(memory_space=pl.ANY)
    dma = pltpu.SemaphoreType.DMA
    results = pl.pallas_call(
        functools.partial(kernel_body, dims, chunks, 1.0 / math.sqrt(total)),
        out_shape=(
            pltpu.VMEM(query_tiles.shape, half),
            pltpu.VMEM(query_tiles.shape, half),
            pltpu.VMEM(query_tiles.shape, half),
            pltpu.VMEM(filters.shape, single),
        ),
        in_specs=[anywhere] * 7,
        out_specs=[anywhere] * 4,
        scratch_shapes=[
            pltpu.VMEM(filters.shape, half),
            pltpu.SMEM(operands[5].shape, jnp.int32),
            pltpu.SMEM(operands[6].shape, jnp.int32),
            pltpu.VMEM((3, slot, features), half),
            pltpu.VMEM((3, chunks, slot, width), half),
            pltpu.VMEM((rows, features), half),
            pltpu.VMEM((tiles, 2 * rows, LANES), half),
            pltpu.VMEM((tiles, 2 * rows, LANES), half),
            pltpu.VMEM((groups * rows, 2 * rows), half),
            pltpu.VMEM((groups * rows, 2 * rows), half),
            pltpu.VMEM((groups * 8, rows), single),
            pltpu.VMEM((groups * 8, rows), single),
            pltpu.VMEM((4, rows, rows), half),
            pltpu.VMEM((4, rows, rows), single),
            pltpu.VMEM((groups * 8, rows), single),
            pltpu.VMEM((groups, rows), single),
            pltpu.VMEM((3, chunks, slot, width), half),
            pltpu.VMEM((3, chunks, slot, width), half),
            pltpu.VMEM((team, piece, rows), single),
            pltpu.VMEM((y_count, piece, rows), single),
            pltpu.VMEM((z_count, piece, rows), single),
            dma((3,)),
            dma((4,)),
            dma((3, chunks)),
            dma((3, chunks)),
            dma((chunks,)),
            dma((chunks,)),
            dma((chunks,)),
            dma((chunks,)),
            dma((3, chunks)),
            dma((3, chunks)),
            dma((3, chunks)),
            dma((team - 1,)),
            dma((team - 1,)),
            dma((y_count - 1,)),
            dma((y_count - 1,)),
            dma((z_count - 1,)),
            dma((z_count - 1,)),
            dma((team - 1,)),
            dma((team - 1,)),
            dma,
        ],
        compiler_params=pltpu.CompilerParams(
            collective_id=0, has_side_effects=True, vmem_limit_bytes=VMEM_BYTES
        ),
        cost_estimate=pl.CostEstimate(
            flops=12 * rows * rows * features, bytes_accessed=14 * rows * features, transcendentals=0
        ),
    )(*operands)
    count = len(results)
    return pl.pallas_call(
        functools.partial(hand_over, count),
        out_shape=tuple(jax.ShapeDtypeStruct(r.shape, r.dtype) for r in results),
        in_specs=[anywhere] * count,
        out_specs=[anywhere] * count,
        scratch_shapes=[dma((2 * count,))],
        compiler_params=pltpu.CompilerParams(vmem_limit_bytes=2 * 1024 * 1024),
    )(*results)


def build(mesh, dims, chunks):
    placed = (
        P("dp", "seq", None, None, None),
        P("dp", "seq", None, None, None),
        P("dp", "seq", None, None, None),
        P("dp", "seq", None),
        P(),
        P(),
        P(None, "seq", None),
    )
    return jax.shard_map(
        functools.partial(body, dims, chunks),
        mesh=mesh,
        in_specs=placed,
        out_specs=(
            P("dp", "seq", None, None, None),
            P("dp", "seq", None, None, None),
            P("dp", "seq", None, None, None),
            P(),
        ),
        check_vma=False,
    )


def solution(mesh):
    return build(mesh, (8, 4, 4), 8)
```

```python
import functools
import math

import jax
import jax.numpy as jnp
from jax import lax
from jax.experimental import pallas as pl
from jax.experimental.pallas import tpu as pltpu
from jax.sharding import PartitionSpec as P

MESH = pl.DeviceIdType.MESH
LANES = 128
VMEM_BYTES = 60 * 1024 * 1024


def kernel_body(
    dims,
    chunks,
    scale,
    query_hbm,
    key_hbm,
    value_hbm,
    cot_hbm,
    filters_hbm,
    doc_hbm,
    arrival_hbm,
    gq_hbm,
    gk_hbm,
    gv_hbm,
    gf_hbm,
    filters_ref,
    doc_ref,
    arrival_ref,
    own,
    rcv,
    cot,
    mixx,
    ggx,
    taps_fwd,
    taps_back,
    rolled_fwd,
    rolled_back,
    masks_half,
    masks,
    diag,
    terms,
    stage_own,
    stage_oth,
    piece_one,
    piece_two,
    small_sem,
    own_sem,
    swap_send,
    swap_recv,
    mix_send,
    mix_recv,
    gg_send,
    gg_recv,
    out_sem,
    back_send,
    back_recv,
    one_send,
    one_recv,
    two_send,
    two_recv,
    four_send,
    four_recv,
    final_sem,
):
    z_count, y_count, x_count = dims
    seq_count = z_count * y_count * x_count
    group_count, kernel = filters_ref.shape
    rows = kernel
    slot = rcv.shape[2]
    width = rcv.shape[3]
    tile_count = mixx.shape[0]
    per_chunk = tile_count // chunks
    per_tile = group_count // tile_count
    group_size = LANES // per_tile
    half_chunks = chunks // 2
    core = lax.axis_index("dp")
    other = 1 - core
    seq = lax.axis_index("seq")
    x = lax.rem(seq, x_count)
    y = lax.rem(lax.div(seq, x_count), y_count)
    z = lax.div(seq, x_count * y_count)
    sibling = (other, seq)
    following = (core, lax.rem(seq + 1, seq_count))
    previous = (core, lax.rem(seq + seq_count - 1, seq_count))
    y_low, y_high = lax.rem(y, 2), lax.div(y, 2)
    pairs = y_count // 2
    team = 4 * x_count
    place = (core * 2 + y_low) * x_count + x
    across_count = pairs * z_count
    across_place = y_high * z_count + z

    def member(k, back=False):
        steps = k % x_count
        here_x = lax.rem(x + (x_count - steps if back else steps), x_count)
        here_low = lax.rem(y_low + (k // x_count) % 2, 2)
        here_core = core if k < 2 * x_count else other
        index = (here_core * 2 + here_low) * x_count + here_x
        return index, (here_core, seq + (here_x - x) + (here_low - y_low) * x_count)

    def across(k, back=False):
        steps, turns = k % z_count, k // z_count
        here_z = lax.rem(z + (z_count - steps if back else steps), z_count)
        here_high = lax.rem(y_high + (pairs - turns if back else turns), pairs)
        apart = (here_z - z) * (x_count * y_count) + (here_high - y_high) * (2 * x_count)
        return here_high * z_count + here_z, (core, seq + apart)

    def hops(ring, k):
        if ring is member:
            steps = k % x_count
            return min(steps, x_count - steps) + (k // x_count) % 2
        steps = k % z_count
        return min(steps, z_count - steps) + 2 * (k // z_count)

    def order(ring, count):
        return sorted(range(1, count), key=lambda k: -hops(ring, k))

    def columns(c):
        return pl.ds(pl.multiple_of(c * width, width), width)

    barrier = pltpu.get_barrier_semaphore()
    partners = [across(k)[1] for k in order(across, across_count)]
    partners += [following, previous]
    partners += [member(k)[1] for k in order(member, team)]
    partners += [sibling]
    for partner in partners:
        pl.semaphore_signal(barrier, inc=1, device_id=partner, device_id_type=MESH)

    small = [
        pltpu.make_async_copy(doc_hbm, doc_ref, small_sem.at[0]),
        pltpu.make_async_copy(filters_hbm, filters_ref, small_sem.at[1]),
        pltpu.make_async_copy(arrival_hbm, arrival_ref, small_sem.at[2]),
    ]
    for copy in small:
        copy.start()

    sources = (key_hbm, value_hbm, query_hbm)

    def chunk_of(which, c):
        return chunks - 1 - c if which == 2 else c

    own_copies = [
        pltpu.make_async_copy(sources[which].at[0, 0, core], own.at[which], own_sem.at[which])
        for which in range(3)
    ]
    own_copies.append(pltpu.make_async_copy(cot_hbm.at[0], cot, own_sem.at[3]))
    for copy in own_copies:
        copy.start()

    def swap_copy(which, c):
        return pltpu.make_async_remote_copy(
            src_ref=sources[which].at[0, 0, other, :, columns(c)],
            dst_ref=rcv.at[which, c],
            send_sem=swap_send.at[which, c],
            recv_sem=swap_recv.at[which, c],
            device_id=sibling,
            device_id_type=MESH,
        )

    pl.semaphore_wait(barrier, len(partners))

    def swap(c):
        for which in range(3):
            swap_copy(which, chunk_of(which, c)).start()

    ahead = 2
    for c in range(ahead):
        swap(c)
    for copy in small:
        copy.wait()

    square = (rows, rows)
    row = lax.broadcasted_iota(jnp.int32, square, 0)
    col = lax.broadcasted_iota(jnp.int32, square, 1)
    first = seq * rows

    def doc_start(position):
        end = jnp.int32(0)
        result = jnp.zeros(square, jnp.int32)
        for i in range(doc_ref.shape[1]):
            length = doc_ref[core, i]
            end = end + length
            result = result + jnp.where(position >= end, length, 0)
        return result

    def as_mask(condition):
        return jnp.where(condition, 1.0, 0.0).astype(jnp.float32)

    start_row = doc_start(first + row)
    start_col = doc_start(first + col)
    start_far = doc_start(first + rows + col)
    built = (
        as_mask((col > row) & (first - rows + col >= start_row)),
        as_mask((col <= row) & (first + col >= start_row)),
        as_mask((col >= row) & (first + row >= start_col)),
        as_mask((col < row) & (first + row >= start_far)),
    )
    for i, mask in enumerate(built):
        masks[i] = mask
        masks_half[i] = mask.astype(jnp.bfloat16)

    flip = as_mask(lax.rem(row + col, kernel) == 0)

    straight = filters_ref[...].astype(jnp.float32)
    turned = jnp.dot(
        filters_ref[...], flip.astype(jnp.bfloat16), preferred_element_type=jnp.float32
    )
    for s in range(8):
        rolled_fwd[pl.ds(s, group_count, stride=8), :] = pltpu.roll(turned, s, 1)
        rolled_back[pl.ds(s, group_count, stride=8), :] = pltpu.roll(straight, s, 1)

    for copy in own_copies:
        copy.wait()

    held = arrival_ref[core, 0, core]
    own_first = jnp.full((slot, LANES), held, jnp.int32) == 0

    def in_order(mine, received):
        return jnp.concatenate(
            [jnp.where(own_first, mine, received), jnp.where(own_first, received, mine)], axis=0
        )

    def halo_mix(c):
        tiles = pl.ds(c * per_chunk, per_chunk)
        return pltpu.make_async_remote_copy(
            src_ref=mixx.at[tiles, pl.ds(rows, rows), :],
            dst_ref=mixx.at[tiles, pl.ds(0, rows), :],
            send_sem=mix_send.at[c],
            recv_sem=mix_recv.at[c],
            device_id=following,
            device_id_type=MESH,
        )

    def halo_gg(c):
        tiles = pl.ds(c * per_chunk, per_chunk)
        return pltpu.make_async_remote_copy(
            src_ref=ggx.at[tiles, pl.ds(0, rows), :],
            dst_ref=ggx.at[tiles, pl.ds(rows, rows), :],
            send_sem=gg_send.at[c],
            recv_sem=gg_recv.at[c],
            device_id=previous,
            device_id_type=MESH,
        )

    mix_turns = (x == x_count - 1) & (y == y_count - 1)
    gg_turns = (x == 0) & (y == 0)

    def halos(first, last, turning):
        @pl.when(mix_turns == turning)
        def _():
            for c in range(first, last):
                halo_mix(c).start()

        @pl.when(gg_turns == turning)
        def _():
            for c in range(first, last):
                halo_gg(chunks - 1 - c).start()

    def lanes_of(c, q):
        return pl.ds(pl.multiple_of(c * width + q * LANES, LANES), LANES)

    plain = (3 * chunks // 4, 7 * chunks // 8, chunks)
    turned = (3 * chunks // 4, 7 * chunks // 8, chunks)

    def assemble(c, carry):
        back = chunks - 1 - c

        @pl.when(c + ahead < chunks)
        def _():
            swap(c + ahead)

        for which in range(2):
            swap_copy(which, c).wait_recv()
        for q in range(per_chunk):
            lanes = slice(q * LANES, (q + 1) * LANES)
            here = lanes_of(c, q)
            mine = own[0, :, here].astype(jnp.float32) * own[1, :, here].astype(jnp.float32)
            received = rcv[0, c, :, lanes].astype(jnp.float32) * rcv[1, c, :, lanes].astype(
                jnp.float32
            )
            mixx[c * per_chunk + q, rows:, :] = in_order(mine, received).astype(jnp.bfloat16)

        @pl.when(c < jnp.where(mix_turns, turned[0], plain[0]))
        def _():
            halo_mix(c).start()

        swap_copy(2, back).wait_recv()
        for q in range(per_chunk):
            lanes = slice(q * LANES, (q + 1) * LANES)
            here = lanes_of(back, q)
            gate = in_order(
                own[2, :, here].astype(jnp.float32), rcv[2, back, :, lanes].astype(jnp.float32)
            )
            ggx[back * per_chunk + q, :rows, :] = (
                gate * cot[:, here].astype(jnp.float32)
            ).astype(jnp.bfloat16)

        @pl.when(c < jnp.where(gg_turns, turned[0], plain[0]))
        def _():
            halo_gg(back).start()

        return carry

    lax.fori_loop(0, chunks, assemble, 0)

    def band(g, carry):
        base = pl.multiple_of(g * rows, rows)
        eight = pl.ds(pl.multiple_of(g * 8, 8), 8)
        for rolled, out, near, far in (
            (rolled_fwd, taps_fwd, 0, 1),
            (rolled_back, taps_back, 2, 3),
        ):
            start = rolled[eight, :]
            whole = jnp.concatenate(
                [start if k == 0 else pltpu.roll(start, 8 * k, 1) for k in range(rows // 8)],
                axis=0,
            ).astype(jnp.bfloat16)
            out[pl.ds(base, rows), :rows] = whole * masks_half[near]
            out[pl.ds(base, rows), rows:] = whole * masks_half[far]
        return carry

    lax.fori_loop(0, group_count, band, 0, unroll=8)

    lane_group = lax.div(lax.broadcasted_iota(jnp.int32, square, 1), group_size)

    def pick(parts):
        result = parts[:rows]
        for j in range(1, per_tile):
            result = jnp.where(lane_group == j, parts[j * rows : (j + 1) * rows], result)
        return result

    def spread(block):
        return jnp.concatenate(
            [
                block * jnp.where(lane_group == j, 1.0, 0.0).astype(jnp.bfloat16)
                for j in range(per_tile)
            ],
            axis=0,
        )

    def split(result):
        top, bottom = result[:slot], result[slot:]
        return jnp.where(own_first, top, bottom), jnp.where(own_first, bottom, top)

    def correlate(tile, left, right, near, far):
        product = lax.dot_general(
            spread(left), right, (((1,), (1,)), ((), ())), preferred_element_type=jnp.float32
        )
        for j in range(per_tile):
            total = None
            for k in range(rows // 8):
                here = slice(j * rows + 8 * k, j * rows + 8 * k + 8)
                mask_rows = slice(8 * k, 8 * k + 8)
                part = (
                    product[here, :rows] * masks[near, mask_rows]
                    + product[here, rows:] * masks[far, mask_rows]
                )
                if k:
                    part = pltpu.roll(part, rows - 8 * k, 1)
                total = part if total is None else total + part
            diag[pl.ds(pl.multiple_of((tile * per_tile + j) * 8, 8), 8), :] = total

    def forward(c, q):
        tile = c * per_chunk + q
        lanes = pl.ds(pl.multiple_of(q * LANES, LANES), LANES)
        lhs = taps_fwd[pl.ds(pl.multiple_of(tile * per_tile * rows, rows), per_tile * rows), :]
        hidden = pick(jnp.dot(lhs, mixx[tile], preferred_element_type=jnp.float32))
        mine, theirs = split(cot[:, lanes_of(c, q)].astype(jnp.float32) * hidden)
        stage_own[2, c, :, lanes] = mine.astype(jnp.bfloat16)
        stage_oth[2, c, :, lanes] = theirs.astype(jnp.bfloat16)

    def backward(c, q):
        tile = c * per_chunk + q
        lanes = pl.ds(pl.multiple_of(q * LANES, LANES), LANES)
        lhs = taps_back[pl.ds(pl.multiple_of(tile * per_tile * rows, rows), per_tile * rows), :]
        grad = pick(jnp.dot(lhs, ggx[tile], preferred_element_type=jnp.float32))
        mine, theirs = split(grad)
        for which in range(2):
            factor = 1 - which
            stage_own[which, c, :, lanes] = (
                mine * own[factor, :, lanes_of(c, q)].astype(jnp.float32)
            ).astype(jnp.bfloat16)
            stage_oth[which, c, :, lanes] = (
                theirs * rcv[factor, c, :, lanes].astype(jnp.float32)
            ).astype(jnp.bfloat16)

    results = (gk_hbm, gv_hbm, gq_hbm)

    def out_copy(which, c):
        return pltpu.make_async_copy(
            stage_own.at[which, c],
            results[which].at[0, 0, core, :, columns(c)],
            out_sem.at[which, c],
        )

    def back_copy(which, c):
        return pltpu.make_async_remote_copy(
            src_ref=stage_oth.at[which, c],
            dst_ref=results[which].at[0, 0, core, :, columns(c)],
            send_sem=back_send.at[which, c],
            recv_sem=back_recv.at[which, c],
            device_id=sibling,
            device_id_type=MESH,
        )

    def arrived(c):
        halo_mix(c).wait_recv()
        halo_gg(chunks - 1 - c).wait_recv()

    def terms_step(c, carry):
        back = chunks - 1 - c
        arrived(c)

        def inner(q, inner_carry):
            tile = c * per_chunk + q
            correlate(tile, ggx[tile, :rows, :], mixx[tile], 0, 1)
            tile = back * per_chunk + q
            correlate(tile, mixx[tile, rows:, :], ggx[tile], 2, 3)
            return inner_carry

        lax.fori_loop(0, per_chunk, inner, 0, unroll=True)
        return carry

    def step(c, carry):
        back = chunks - 1 - c

        @pl.when(c >= half_chunks)
        def _():
            arrived(c)

        def inner(q, inner_carry):
            forward(c, q)
            backward(back, q)
            return inner_carry

        lax.fori_loop(0, per_chunk, inner, 0, unroll=True)
        for which, chunk in ((2, c), (0, back), (1, back)):
            out_copy(which, chunk).start()
            back_copy(which, chunk).start()
        return carry

    before = chunks // 4
    lax.fori_loop(0, half_chunks - 1, terms_step, 0)
    lax.fori_loop(0, before, step, 0)
    terms_step(half_chunks - 1, 0)

    reversed_half = group_count // 2
    sums = None
    for s in range(8):
        part = diag[pl.ds(s, group_count, stride=8), :]
        if s:
            part = pltpu.roll(part, rows - s, 1)
        sums = part if sums is None else sums + part
    terms[:reversed_half, :] = jnp.dot(
        sums[:reversed_half],
        flip,
        precision=lax.Precision.HIGHEST,
        preferred_element_type=jnp.float32,
    )
    terms[reversed_half:, :] = sums[reversed_half:]
    piece = group_count // team

    def piece_rows(index):
        return pl.ds(pl.multiple_of(index * piece, piece), piece)

    def remote(src, dst, send, recv, device):
        return pltpu.make_async_remote_copy(
            src_ref=src,
            dst_ref=dst,
            send_sem=send,
            recv_sem=recv,
            device_id=device,
            device_id_type=MESH,
        )

    def exchange(ring, count, here, buffer, source, send, recv):
        copies = []
        for k in order(ring, count):
            index, device = ring(k)
            copy = remote(
                source(index), buffer.at[here], send.at[k - 1], recv.at[k - 1], device
            )
            copy.start()
            copies.append(copy)
        return copies

    def arrive(ring, count, buffer, send, recv):
        for k in range(1, count):
            index, device = ring(k, back=True)
            remote(
                buffer.at[index], buffer.at[index], send.at[k - 1], recv.at[k - 1], device
            ).wait_recv()

    def total_of(buffer, count):
        total = buffer[0]
        for k in range(1, count):
            total = total + buffer[k]
        return total

    own_piece = pltpu.make_async_copy(
        diag.at[piece_rows(place)], gf_hbm.at[piece_rows(place)], final_sem
    )
    sent = []
    piece_one[place] = terms[piece_rows(place), :]
    sent += exchange(
        member, team, place, piece_one, lambda i: terms.at[piece_rows(i)], one_send, one_recv
    )

    def advance(stage):
        if stage == 0:
            arrive(member, team, piece_one, one_send, one_recv)
            piece_two[across_place] = total_of(piece_one, team)
            return exchange(
                across,
                across_count,
                across_place,
                piece_two,
                lambda i: piece_two.at[across_place],
                two_send,
                two_recv,
            )
        if stage == 1:
            arrive(across, across_count, piece_two, two_send, two_recv)
            diag[piece_rows(place), :] = total_of(piece_two, across_count) * scale
            own_piece.start()
            copies = []
            for k in order(member, team):
                index, device = member(k)
                copy = remote(
                    diag.at[piece_rows(place)],
                    gf_hbm.at[piece_rows(place)],
                    four_send.at[k - 1],
                    four_recv.at[k - 1],
                    device,
                )
                copy.start()
                copies.append(copy)
            return copies
        for k in range(1, team):
            index, device = member(k, back=True)
            remote(
                gf_hbm.at[piece_rows(index)],
                gf_hbm.at[piece_rows(index)],
                four_send.at[k - 1],
                four_recv.at[k - 1],
                device,
            ).wait_recv()
        return []


    def finish(c, carry):
        halo_mix(c).wait_send()
        halo_gg(c).wait_send()
        for which in range(3):
            swap_copy(which, c).wait_send()
            out_copy(which, c).wait()
            back_copy(which, c).wait()
        return carry

    ends = (before, chunks // 2, 7 * chunks // 8, chunks)
    for stage in range(3):
        if stage < 2:
            halos(plain[stage], plain[stage + 1], False)
            halos(turned[stage], turned[stage + 1], True)
        lax.fori_loop(ends[stage], ends[stage + 1], step, 0)
        if stage == 2:
            for copy in sent[: -(team - 1)]:
                copy.wait_send()
            lax.fori_loop(0, chunks, finish, 0)
        sent += advance(stage)
    for copy in sent[-(team - 1) :]:
        copy.wait_send()
    own_piece.wait()


def hand_over(count, *refs):
    copies = []
    for i in range(count):
        source, target, sems = refs[i], refs[count + i], refs[-1]
        if len(source.shape) == 2:
            copies.append(pltpu.make_async_copy(source, target, sems.at[2 * i]))
            continue
        for j in range(2):
            copies.append(
                pltpu.make_async_copy(
                    source.at[0, 0, j], target.at[0, 0, j], sems.at[2 * i + j]
                )
            )
    for copy in copies:
        copy.start()
    for copy in copies:
        copy.wait()


def body(dims, chunks, *operands):
    query_tiles, cotangent, filters = operands[0], operands[3], operands[4]
    slot, features = query_tiles.shape[3:]
    rows = cotangent.shape[1]
    groups = filters.shape[0]
    z_count, y_count, x_count = dims
    team = 4 * x_count
    across_count = y_count // 2 * z_count
    piece = groups // team
    width = features // chunks
    tiles = features // LANES
    half, single = jnp.bfloat16, jnp.float32
    total = 2 * rows * z_count * y_count * x_count * (features // groups)
    anywhere = pl.BlockSpec(memory_space=pl.ANY)
    dma = pltpu.SemaphoreType.DMA
    results = pl.pallas_call(
        functools.partial(kernel_body, dims, chunks, 1.0 / math.sqrt(total)),
        out_shape=(
            pltpu.VMEM(query_tiles.shape, half),
            pltpu.VMEM(query_tiles.shape, half),
            pltpu.VMEM(query_tiles.shape, half),
            pltpu.VMEM(filters.shape, single),
        ),
        in_specs=[anywhere] * 7,
        out_specs=[anywhere] * 4,
        scratch_shapes=[
            pltpu.VMEM(filters.shape, half),
            pltpu.SMEM(operands[5].shape, jnp.int32),
            pltpu.SMEM(operands[6].shape, jnp.int32),
            pltpu.VMEM((3, slot, features), half),
            pltpu.VMEM((3, chunks, slot, width), half),
            pltpu.VMEM((rows, features), half),
            pltpu.VMEM((tiles, 2 * rows, LANES), half),
            pltpu.VMEM((tiles, 2 * rows, LANES), half),
            pltpu.VMEM((groups * rows, 2 * rows), half),
            pltpu.VMEM((groups * rows, 2 * rows), half),
            pltpu.VMEM((groups * 8, rows), single),
            pltpu.VMEM((groups * 8, rows), single),
            pltpu.VMEM((4, rows, rows), half),
            pltpu.VMEM((4, rows, rows), single),
            pltpu.VMEM((groups * 8, rows), single),
            pltpu.VMEM((groups, rows), single),
            pltpu.VMEM((3, chunks, slot, width), half),
            pltpu.VMEM((3, chunks, slot, width), half),
            pltpu.VMEM((team, piece, rows), single),
            pltpu.VMEM((across_count, piece, rows), single),
            dma((3,)),
            dma((4,)),
            dma((3, chunks)),
            dma((3, chunks)),
            dma((chunks,)),
            dma((chunks,)),
            dma((chunks,)),
            dma((chunks,)),
            dma((3, chunks)),
            dma((3, chunks)),
            dma((3, chunks)),
            dma((team - 1,)),
            dma((team - 1,)),
            dma((across_count - 1,)),
            dma((across_count - 1,)),
            dma((team - 1,)),
            dma((team - 1,)),
            dma,
        ],
        compiler_params=pltpu.CompilerParams(
            collective_id=0, has_side_effects=True, vmem_limit_bytes=VMEM_BYTES
        ),
        cost_estimate=pl.CostEstimate(
            flops=12 * rows * rows * features, bytes_accessed=14 * rows * features, transcendentals=0
        ),
    )(*operands)
    count = len(results)
    return pl.pallas_call(
        functools.partial(hand_over, count),
        out_shape=tuple(jax.ShapeDtypeStruct(r.shape, r.dtype) for r in results),
        in_specs=[anywhere] * count,
        out_specs=[anywhere] * count,
        scratch_shapes=[dma((2 * count,))],
        compiler_params=pltpu.CompilerParams(vmem_limit_bytes=2 * 1024 * 1024),
    )(*results)


def build(mesh, dims, chunks):
    placed = (
        P("dp", "seq", None, None, None),
        P("dp", "seq", None, None, None),
        P("dp", "seq", None, None, None),
        P("dp", "seq", None),
        P(),
        P(),
        P(None, "seq", None),
    )
    return jax.shard_map(
        functools.partial(body, dims, chunks),
        mesh=mesh,
        in_specs=placed,
        out_specs=(
            P("dp", "seq", None, None, None),
            P("dp", "seq", None, None, None),
            P("dp", "seq", None, None, None),
            P(),
        ),
        check_vma=False,
    )


def solution(mesh):
    return build(mesh, (8, 4, 4), 8)
```
